256 devices in a mesh: slab: 16 (over z, core), align: 16 (over y, x).
Axes of the slice: x: 4, y: 4, z: 8, core: 2. Of those that a mesh axis runs over, the one named last changes fastest.
Arguments:
- volume: bfloat16 [256, 256, 512], P('slab', 'align'), may hold values from -6 to 6
- images: bfloat16 [8192, 256, 512], P('slab', 'align'), may hold values from -6 to 6
- orient: int32 [8192, 8], P('slab'), may hold values from 0 to 64
- defocus: bfloat16 [8192], P('slab'), may hold values from 20 to 200
- particle_counts: int32 [16], P('slab'), may hold values from 128 to 512, as said below
Outputs:
- back_projection: float32 [256, 256, 512], P('slab', 'align')
- posterior: float32 [8192, 8], P('slab')
The draws below stay inside these ranges and needn't reach their ends.
Inputs may be any that keep to these rules, and one draw needn't show every extreme that they name: `particle_counts`: some slab index holds 512 live particles in every draw.
All inputs are finite; a program needn't handle non-finite values.
Results may differ from the reference program's by a relative error of at most 0.005.
Values may be sent and summed in bfloat16 or wider, within the bound.
A program may use at most 128 MiB of HBM per device.

```python
import math
import jax
import jax.numpy as jnp
from jax import lax

BOX = 256
TILT_STEPS = 32
GRID = 65
CAND = 8
PART_DEV = 512
PARTICLES = 8192
N_SLAB = 16


def draw_particle_counts(key, part):
    base_counts = jax.random.randint(key, (N_SLAB,), PART_DEV // 4, PART_DEV + 1)
    full_index = jax.random.randint(jax.random.fold_in(key, 7), (), 0, N_SLAB)
    slab_ids = jnp.arange(N_SLAB, dtype=jnp.int32)
    return jnp.where(slab_ids == full_index, PART_DEV, base_counts).astype(jnp.int32)


def set_ends(array, own_key, low, high):
    index_at = [jax.random.randint(jax.random.fold_in(own_key, axis), (), 0, length) for axis, length in enumerate(array.shape)]
    main_axis = array.shape.index(max(array.shape))
    neighbour = index_at[:main_axis] + [(index_at[main_axis] + 1) % array.shape[main_axis]] + index_at[main_axis + 1:]
    return array.at[tuple(index_at)].set(low).at[tuple(neighbour)].set(high)


def level_of(stream_key, shape, split, low, top_value):
    gain, own = 1.0, jax.random.fold_in(stream_key, 6)
    for position, shards_of in split:
        draws = jnp.exp(jax.random.uniform(jax.random.fold_in(own, position), (shards_of,), jnp.float32, low / len(split), top_value / len(split)))
        gain = gain * jnp.repeat(draws, shape[position] // shards_of).reshape([-1 if axis == position else 1 for axis in range(len(shape))])
    return gain


def normal_values(stream_key, dims, spread, most, pieces=(), kind=jnp.bfloat16):
    values = jax.random.normal(stream_key, dims, jnp.float32) * spread
    if len(pieces) > 0:
        values = level_of(stream_key, dims, pieces, -0.22, 0.18) * values
    return jnp.clip(values, min=-most, max=most).astype(kind)


def setup_inputs(seed: int = 0) -> dict:
    key_of = jax.random.split(jax.random.key(seed), 6)
    volume = normal_values(key_of[0], (BOX, BOX, 2 * BOX), 1.0, 6.0, ((0, 16), (1, 16)))
    images = normal_values(key_of[1], (PARTICLES, BOX, 2 * BOX), 1.0, 6.0, ((0, 16), (1, 16)))
    orient = set_ends(jax.random.randint(key_of[2], (PARTICLES, CAND), 0, GRID), jax.random.fold_in(key_of[2], 1), 0, GRID - 1).astype(jnp.int32)
    defocus = jnp.clip(jnp.exp(math.log(200.0) - 2.3025851 * jax.random.uniform(key_of[3], (PARTICLES,), jnp.float32) ** level_of(key_of[3], (PARTICLES,), ((0, 16),), -0.2, 0.2)), 20.0, 200.0).astype(jnp.bfloat16)
    particle_counts = draw_particle_counts(jax.random.fold_in(key_of[5], 71), 0)
    return {"volume": volume, "images": images, "orient": orient, "defocus": defocus, "particle_counts": particle_counts}


ctf_phase = 0.1


def grid_weights(row_first, row_count, plane_first, plane_count):
    tilts = jnp.arange(GRID, dtype=jnp.int32) - TILT_STEPS
    ky_rows = row_first + jnp.arange(row_count, dtype=jnp.int32)
    offset = tilts[:, None] * (ky_rows[None, :] - BOX // 2)
    lower = jnp.mod(BOX // 2 + jnp.floor_divide(offset, TILT_STEPS), BOX)
    upper = jnp.mod(lower + 1, BOX)
    fraction = jnp.mod(offset, TILT_STEPS).astype(jnp.float32) / TILT_STEPS
    planes_here = plane_first + jnp.arange(plane_count, dtype=jnp.int32)
    at_lower = (planes_here[None, None, :] == lower[:, :, None]).astype(jnp.float32)
    at_upper = (planes_here[None, None, :] == upper[:, :, None]).astype(jnp.float32)
    return (1.0 - fraction)[:, :, None] * at_lower + fraction[:, :, None] * at_upper


def contrast(defocus, row_first, row_count):
    ky_rows = (row_first + jnp.arange(row_count, dtype=jnp.int32)).astype(jnp.float32) - BOX / 2
    kx_cols = jnp.arange(BOX, dtype=jnp.int32).astype(jnp.float32) - BOX / 2
    radius = (kx_cols[None, :] * kx_cols[None, :] + ky_rows[:, None] * ky_rows[:, None]) / (BOX * BOX)
    wave = jnp.sin(defocus.astype(jnp.float32)[:, None, None] * radius[None, :, :] + ctf_phase)
    return jnp.concatenate([wave, wave], axis=-1)


def reference(volume, images, orient, defocus, particle_counts):
    weights = grid_weights(0, BOX, 0, BOX)
    projected = jnp.einsum("grz,zrc->grc", weights, volume.astype(jnp.float32), precision=lax.Precision.HIGHEST)
    sections = projected.astype(jnp.bfloat16)
    section_sq = (sections.astype(jnp.float32) * sections.astype(jnp.float32)).astype(jnp.bfloat16)
    flat_sections = sections.reshape(GRID, -1)
    flat_sq = section_sq.reshape(GRID, -1)
    grid_ids = jnp.arange(GRID, dtype=jnp.int32)

    def one_block(summed, block):
        block_images, block_orient, block_defocus, block_count = block
        wave = contrast(block_defocus, 0, BOX)
        weighted = (wave * block_images.astype(jnp.float32)).astype(jnp.bfloat16).reshape(PART_DEV, -1)
        wave_sq = (wave * wave).astype(jnp.bfloat16).reshape(PART_DEV, -1)
        energy = jnp.sum(jnp.square(block_images.astype(jnp.float32)).reshape(PART_DEV, -1), axis=1)
        cross = jnp.dot(weighted, flat_sections.T, preferred_element_type=jnp.float32)
        quad = jnp.dot(wave_sq, flat_sq.T, preferred_element_type=jnp.float32)
        distance = energy[:, None] - 2.0 * cross + quad
        chosen = block_orient[:, :, None] == grid_ids[None, None, :]
        picked = jnp.sum(jnp.where(chosen, distance[:, None, :], jnp.float32(0.0)), axis=-1)
        scores = -picked / BOX
        active = jnp.arange(PART_DEV, dtype=jnp.int32) < block_count
        posterior = jnp.where(active[:, None], jax.nn.softmax(scores, axis=-1), jnp.float32(0.0))
        per_grid = jnp.sum(jnp.where(chosen, posterior[:, :, None], jnp.float32(0.0)), axis=1).astype(jnp.bfloat16)
        summed = summed + jnp.dot(per_grid.T, weighted, preferred_element_type=jnp.float32)
        return summed, posterior

    blocks = (images.reshape(N_SLAB, PART_DEV, BOX, 2 * BOX), orient.reshape(N_SLAB, PART_DEV, CAND),
              defocus.reshape(N_SLAB, PART_DEV), particle_counts)
    summed, posteriors = lax.scan(one_block, jnp.zeros((GRID, BOX * 2 * BOX), jnp.float32), blocks)
    back_projection = jnp.einsum("grz,grc->zrc", weights, summed.reshape(GRID, BOX, 2 * BOX), precision=lax.Precision.HIGHEST)
    return back_projection, posteriors.reshape(PARTICLES, CAND)
```

```python
import functools

import jax
import jax.numpy as jnp
from jax import lax
from jax.experimental import pallas as pl
from jax.experimental.pallas import tpu as pltpu
from jax.sharding import PartitionSpec as P

BOX = 256
TILT_STEPS = 32
GRID = 65
CAND = 8
GPAD = 80
BLOCK = 16
ROWS = 16
CHIPS = 8
CTF_PHASE = 0.1
MESH = pl.DeviceIdType.MESH
BF16 = jnp.bfloat16
F32 = jnp.float32


def first_row(align):
    return align * ROWS


def sin_cos(angle):
    turns = jnp.floor(angle * F32(0.15915494309189535) + F32(0.5))
    half = ((angle - turns * F32(6.28125)) - turns * F32(0.0019353071795864769)) * F32(0.5)
    sq = half * half
    s = F32(-1.0 / 39916800.0)
    for coefficient in (1.0 / 362880.0, -1.0 / 5040.0, 1.0 / 120.0, -1.0 / 6.0, 1.0):
        s = s * sq + F32(coefficient)
    s = s * half
    c = F32(1.0 / 479001600.0)
    for coefficient in (-1.0 / 3628800.0, 1.0 / 40320.0, -1.0 / 720.0, 1.0 / 24.0, -0.5, 1.0):
        c = c * sq + F32(coefficient)
    return F32(2.0) * s * c, F32(1.0) - F32(2.0) * s * s


def tilt_weights(g, plane, ky):
    offset = (g - TILT_STEPS) * (ky - BOX // 2)
    lower = (BOX // 2 + lax.shift_right_arithmetic(offset, 5)) & (BOX - 1)
    upper = (lower + 1) & (BOX - 1)
    fraction = (offset & (TILT_STEPS - 1)).astype(F32) * F32(1.0 / TILT_STEPS)
    zero = jnp.zeros_like(fraction)
    weights = jnp.where(plane == lower, F32(1.0) - fraction, zero) + jnp.where(plane == upper, fraction, zero)
    return weights.astype(BF16)


def iota(shape, axis):
    return lax.broadcasted_iota(jnp.int32, shape, axis)


def dot_nt(a, b):
    return lax.dot_general(a, b, (((1,), (1,)), ((), ())), preferred_element_type=F32)


def dot_nn(a, b):
    return jnp.dot(a, b, preferred_element_type=F32)


def kernel(
    n_slab, n_align, meta_ref, vol_ref, img_ref, bp_ref, post_ref,
    img_buf, lhs, perm, volt, planes, sec, dist, energy, pick,
    osum, psend, precv, up_send, up_recv, dn_send, dn_recv, bsend, brecv,
    img_sem, a2a_send, a2a_recv, up_ss, up_rs, dn_ss, dn_rs, pt_ss, pt_rs,
    ps_ss, ps_rs, rp_ss, rp_rs, ru_ss, ru_rs, rd_ss, rd_rs, b_ss, b_rs,
):
    s = lax.axis_index("slab")
    a = lax.axis_index("align")
    z = lax.div(s, 2)
    k = lax.rem(s, 2)
    slots = lhs.shape[1]
    cols = 2 * BOX

    def slab_of(offset, core):
        return 2 * lax.rem(z + (offset % CHIPS), CHIPS) + core

    up = (slab_of(1, k), a)
    down = (slab_of(-1, k), a)
    partner = (2 * z + 1 - k, a)

    def remote(src, dst, send, recv, device):
        return pltpu.make_async_remote_copy(
            src_ref=src, dst_ref=dst, send_sem=send, recv_sem=recv, device_id=device, device_id_type=MESH
        )

    barrier = pltpu.get_barrier_semaphore()
    for i in range(1, n_slab):
        pl.semaphore_signal(barrier, inc=1, device_id=(lax.rem(s + i, n_slab), a), device_id_type=MESH)
    for i in range(1, n_align):
        pl.semaphore_signal(barrier, inc=1, device_id=(s, lax.rem(a + i, n_align)), device_id_type=MESH)

    n_chunks = img_sem.shape[0]
    chunk = slots // n_chunks

    def image_copy(i):
        part = pl.ds(i * chunk, chunk)
        return pltpu.make_async_copy(img_ref.at[part], img_buf.at[part], img_sem.at[i])

    for i in range(n_chunks):
        image_copy(i).start()

    r = iota((256, 256), 0)
    c = iota((256, 256), 1)
    swap = (lax.shift_right_logical(r, 4) == (c & 15)) & ((r & 15) == lax.shift_right_logical(c, 4))
    perm[...] = jnp.where(swap, F32(1.0), F32(0.0)).astype(BF16)
    volt[...] = dot_nn(perm[...], vol_ref[...].reshape(256, cols)).astype(BF16).reshape(ROWS, 16, cols)

    pl.semaphore_wait(barrier, n_slab + n_align - 2)

    def plane_copy(i):
        to = lax.rem(s + i, n_slab)
        return remote(volt.at[to], planes.at[s], a2a_send.at[i], a2a_recv.at[i], (to, a))

    for i in range(1, n_slab):
        plane_copy(i).start()
    planes[s] = volt[s]

    kx = (iota((BLOCK, BOX), 1) - BOX // 2).astype(F32)
    kx2 = kx * kx * F32(1.0 / (BOX * BOX))
    ky = ((iota((BLOCK, 128), 1) & (ROWS - 1)) + first_row(a) - BOX // 2).astype(F32)
    ky2 = ky * ky * F32(1.0 / (BOX * BOX))

    @pl.loop(0, n_chunks)
    def _(i):
        image_copy(i).wait()

        @pl.loop(0, chunk // BLOCK)
        def _(j):
            at = pl.ds(pl.multiple_of(i * chunk + j * BLOCK, BLOCK), BLOCK)
            defocus = meta_ref[at, :].astype(F32)[:, CAND : CAND + 1]
            sin_x, cos_x = sin_cos(defocus * kx2)
            sin_y, cos_y = sin_cos(defocus * ky2 + F32(CTF_PHASE))
            rows = dot_nn(perm[...], img_buf[at].reshape(256, cols))
            total = jnp.zeros((BLOCK, BOX), F32)
            for row in range(ROWS):
                wave = sin_x * cos_y[:, row : row + 1] + cos_x * sin_y[:, row : row + 1]
                real = rows[row * BLOCK : (row + 1) * BLOCK, :BOX]
                imag = rows[row * BLOCK : (row + 1) * BLOCK, BOX:]
                total = total + (real * real + imag * imag)
                lhs[row, at, 0:BOX] = (wave * real).astype(BF16)
                lhs[row, at, BOX:cols] = (wave * imag).astype(BF16)
                lhs[row, at, cols : cols + BOX] = (wave * wave).astype(BF16)
            energy[at, :] = total[:, :128] + total[:, 128:]

    for i in range(1, n_slab):
        plane_copy(i).wait_recv()
    weights = tilt_weights(iota((GPAD, BOX), 0), iota((GPAD, BOX), 1), first_row(a) + s)
    projected = dot_nn(weights, planes[...].reshape(BOX, cols)).astype(BF16)
    sec[s, 0] = projected[:, :BOX]
    sec[s, 1] = projected[:, BOX:]

    def sec_up(step, h):
        row = slab_of(-(step - 1), k)
        return remote(sec.at[row, h], sec.at[row, h], up_ss.at[step - 1, h], up_rs.at[step - 1, h], up)

    def sec_down(step, h):
        row = slab_of(step - 1, k)
        return remote(sec.at[row, h], sec.at[row, h], dn_ss.at[step - 1, h], dn_rs.at[step - 1, h], down)

    def sec_partner(offset, h):
        row = slab_of(offset, k)
        slot = offset % CHIPS
        return remote(sec.at[row, h], sec.at[row, h], pt_ss.at[slot, h], pt_rs.at[slot, h], partner)

    def has_up(step, h):
        return step <= 3 or (step == 4 and h == 0)

    def has_down(step, h):
        return step <= 3 or (step == 4 and h == 1)

    for h in range(2):
        sec_up(1, h).start()
        sec_down(1, h).start()
    for h in range(2):
        sec_partner(0, h).start()

    dist[...] = jnp.zeros_like(dist)

    def score(row):
        real = sec[row, 0].astype(F32)
        imag = sec[row, 1].astype(F32)
        square = (real * real + imag * imag).astype(BF16)
        dist[:, :GPAD] += (
            dot_nt(lhs[row, :, 0:BOX], (real * F32(-2.0)).astype(BF16))
            + dot_nt(lhs[row, :, BOX:cols], (imag * F32(-2.0)).astype(BF16))
            + dot_nt(lhs[row, :, cols : cols + BOX], square)
        )

    score(s)
    for step in range(1, 5):
        for h in range(2):
            if has_up(step, h):
                sec_up(step, h).wait_recv()
                if has_up(step + 1, h):
                    sec_up(step + 1, h).start()
                sec_partner(-step, h).start()
            if has_down(step, h):
                sec_down(step, h).wait_recv()
                if has_down(step + 1, h):
                    sec_down(step + 1, h).start()
                sec_partner(step, h).start()
        past = [0] if step == 1 else [-(step - 1), step - 1]
        for offset in past:
            for h in range(2):
                sec_partner(offset, h).wait_recv()

        @pl.loop(0, len(past))
        def _(i):
            score(2 * lax.rem(z + CHIPS + (2 * i - 1) * (step - 1), CHIPS) + 1 - k)

        now = [4] if step == 4 else [-step, step]

        @pl.loop(0, len(now))
        def _(i):
            score(2 * lax.rem(z + CHIPS + (2 * i - 1) * step, CHIPS) + k)

    for h in range(2):
        sec_partner(4, h).wait_recv()
    score(slab_of(4, 1 - k))

    meta_t = dot_nt((iota((16, 16), 0) == iota((16, 16), 1)).astype(F32).astype(BF16), meta_ref[...])
    full = dist[...] + jnp.sum(energy[...], axis=1, keepdims=True)
    full_t = full.T[:GPAD]
    g_ids = iota((GPAD, slots), 0).astype(F32)
    for n in range(CAND):
        chosen = meta_t[n : n + 1, :] == g_ids
        pick[a, n : n + 1, :] = jnp.sum(jnp.where(chosen, full_t, F32(0.0)), axis=0, keepdims=True)

    def pick_copy(i):
        to = lax.rem(a + i, n_align)
        return remote(pick.at[a], pick.at[a], ps_ss.at[i], ps_rs.at[i], (s, to))

    for i in range(1, n_align):
        pick_copy(i).start()
    for i in range(1, n_align):
        pick_copy(i).wait_recv()
    picked = pick[0]
    for i in range(1, n_align):
        picked = picked + pick[i]
    scores = picked * F32(-1.0 / BOX)
    e = jnp.exp(scores - jnp.max(scores, axis=0, keepdims=True))
    posterior = e / jnp.sum(e, axis=0, keepdims=True)
    posterior = jnp.where(meta_t[CAND + 1 : CAND + 2, :] > F32(0.5), posterior, F32(0.0))
    post_ref[...] = posterior
    per_grid = jnp.zeros((GPAD, slots), F32)
    for n in range(CAND):
        chosen = meta_t[n : n + 1, :] == g_ids
        per_grid = per_grid + jnp.where(chosen, posterior[n : n + 1, :], F32(0.0))
    per_grid = per_grid.astype(BF16)

    def summed(row):
        return dot_nn(per_grid, lhs[row, :, 0:cols])

    def pair_copy(i):
        return remote(psend.at[i], precv.at[i], rp_ss.at[i], rp_rs.at[i], partner)

    offsets = [4, 3, 5, 2, 6, 1, 7, 0]

    def produce(i):
        psend[i] = summed(slab_of(offsets[i], 1 - k)).astype(BF16)
        pair_copy(i).start()
        osum[i] = summed(slab_of(offsets[i], k))

    def ring_up(step, h):
        return remote(
            up_send.at[step, h], up_recv.at[step, h], ru_ss.at[step, h], ru_rs.at[step, h], up
        )

    def ring_down(step, h):
        return remote(
            dn_send.at[step, h], dn_recv.at[step, h], rd_ss.at[step, h], rd_rs.at[step, h], down
        )

    def half(h):
        return slice(h * BOX, (h + 1) * BOX)

    def pair_sum(i, h):
        return osum[i, :, half(h)] + precv[i, :, half(h)].astype(F32)

    produce(0)
    produce(1)
    produce(2)
    pair_copy(0).wait_recv()
    up_send[0, 0] = pair_sum(0, 0).astype(BF16)
    ring_up(0, 0).start()
    dn_send[0, 1] = pair_sum(0, 1).astype(BF16)
    ring_down(0, 1).start()
    for step in range(1, 4):
        if step == 1:
            pair_copy(1).wait_recv()
            up_send[1, 1] = pair_sum(1, 1).astype(BF16)
            ring_up(1, 1).start()
            pair_copy(2).wait_recv()
            dn_send[1, 0] = pair_sum(2, 0).astype(BF16)
            ring_down(1, 0).start()
        else:
            pair_copy(2 * step - 1).wait_recv()
            pair_copy(2 * step).wait_recv()
        if step < 3:
            produce(2 * step + 1)
            produce(2 * step + 2)
        else:
            produce(7)
        for h in range(2):
            if step > 1 or h == 0:
                ring_up(step - 1, h).wait_recv()
                up_send[step, h] = (pair_sum(2 * step - 1, h) + up_recv[step - 1, h].astype(F32)).astype(BF16)
                ring_up(step, h).start()
            if step > 1 or h == 1:
                ring_down(step - 1, h).wait_recv()
                dn_send[step, h] = (pair_sum(2 * step, h) + dn_recv[step - 1, h].astype(F32)).astype(BF16)
                ring_down(step, h).start()
    pair_copy(7).wait_recv()
    halves = []
    for h in range(2):
        ring_up(3, h).wait_recv()
        ring_down(3, h).wait_recv()
        halves.append(pair_sum(7, h) + up_recv[3, h].astype(F32) + dn_recv[3, h].astype(F32))

    weights_t = tilt_weights(
        lax.rem(iota((BOX, 2 * GPAD), 1), GPAD), iota((BOX, 2 * GPAD), 0), first_row(a) + s
    )
    for h in range(2):
        high = halves[h].astype(BF16)
        low = (halves[h] - high.astype(F32)).astype(BF16)
        back = dot_nn(weights_t, jnp.concatenate([high, low], axis=0)).astype(BF16)
        bsend[:, :, half(h)] = back.reshape(n_slab, 16, BOX)

    def back_copy(i):
        to = lax.rem(s + i, n_slab)
        return remote(bsend.at[to], brecv.at[s], b_ss.at[i], b_rs.at[i], (to, a))

    for i in range(1, n_slab):
        back_copy(i).start()
    brecv[s] = bsend[s]
    for i in range(1, n_slab):
        back_copy(i).wait_recv()
    bp_ref[...] = dot_nn(perm[...], brecv[...].reshape(256, cols)).reshape(16, ROWS, cols)

    for i in range(1, n_slab):
        plane_copy(i).wait_send()
        back_copy(i).wait_send()
    for i in range(1, n_align):
        pick_copy(i).wait_send()
    for h in range(2):
        for step in range(1, 5):
            if has_up(step, h):
                sec_up(step, h).wait_send()
            if has_down(step, h):
                sec_down(step, h).wait_send()
        for offset in range(CHIPS):
            sec_partner(offset, h).wait_send()
        for step in range(4):
            if step > 0 or h == 0:
                ring_up(step, h).wait_send()
            if step > 0 or h == 1:
                ring_down(step, h).wait_send()
    for i in range(CHIPS):
        pair_copy(i).wait_send()


def on_device(n_slab, n_align, volume, images, orient, defocus, particle_counts):
    slots = images.shape[0]
    cols = 2 * BOX
    active = jnp.arange(slots, dtype=jnp.int32) < particle_counts[0]
    meta = jnp.concatenate(
        [
            orient.astype(BF16),
            defocus[:, None],
            active[:, None].astype(BF16),
            jnp.zeros((slots, 16 - CAND - 2), BF16),
        ],
        axis=1,
    )
    n_chunks = 8 if slots >= 128 else 1
    dma = pltpu.SemaphoreType.DMA
    vmem = pl.BlockSpec(memory_space=pltpu.VMEM)
    back_projection, posterior = pl.pallas_call(
        functools.partial(kernel, n_slab, n_align),
        out_shape=(
            jax.ShapeDtypeStruct((16, ROWS, cols), F32),
            jax.ShapeDtypeStruct((CAND, slots), F32),
        ),
        in_specs=[vmem, vmem, pl.BlockSpec(memory_space=pl.ANY)],
        out_specs=(vmem, vmem),
        scratch_shapes=[
            pltpu.VMEM((slots, ROWS, cols), BF16),
            pltpu.VMEM((ROWS, slots, cols + BOX), BF16),
            pltpu.VMEM((256, 256), BF16),
            pltpu.VMEM((ROWS, 16, cols), BF16),
            pltpu.VMEM((n_slab, 16, cols), BF16),
            pltpu.VMEM((ROWS, 2, GPAD, BOX), BF16),
            pltpu.VMEM((slots, 128), F32),
            pltpu.VMEM((slots, 128), F32),
            pltpu.VMEM((n_align, CAND, slots), F32),
            pltpu.VMEM((CHIPS, GPAD, cols), F32),
            pltpu.VMEM((CHIPS, GPAD, cols), BF16),
            pltpu.VMEM((CHIPS, GPAD, cols), BF16),
            pltpu.VMEM((4, 2, GPAD, BOX), BF16),
            pltpu.VMEM((4, 2, GPAD, BOX), BF16),
            pltpu.VMEM((4, 2, GPAD, BOX), BF16),
            pltpu.VMEM((4, 2, GPAD, BOX), BF16),
            pltpu.VMEM((n_slab, 16, cols), BF16),
            pltpu.VMEM((n_slab, 16, cols), BF16),
            dma((n_chunks,)),
            dma((n_slab,)),
            dma((n_slab,)),
            dma((4, 2)),
            dma((4, 2)),
            dma((4, 2)),
            dma((4, 2)),
            dma((CHIPS, 2)),
            dma((CHIPS, 2)),
            dma((n_align,)),
            dma((n_align,)),
            dma((CHIPS,)),
            dma((CHIPS,)),
            dma((4, 2)),
            dma((4, 2)),
            dma((4, 2)),
            dma((4, 2)),
            dma((n_slab,)),
            dma((n_slab,)),
        ],
        compiler_params=pltpu.CompilerParams(
            collective_id=0, has_side_effects=True, vmem_limit_bytes=48 * 1024 * 1024
        ),
    )(meta, volume, images)
    return back_projection, posterior.T


def solution(mesh):
    return jax.shard_map(
        functools.partial(on_device, mesh.shape["slab"], mesh.shape["align"]),
        mesh=mesh,
        in_specs=(
            P("slab", "align", None),
            P("slab", "align", None),
            P("slab", None),
            P("slab"),
            P("slab"),
        ),
        out_specs=(P("slab", "align", None), P("slab", None)),
        check_vma=False,
    )
```

```python
import functools

import jax
import jax.numpy as jnp
from jax import lax
from jax.experimental import pallas as pl
from jax.experimental.pallas import tpu as pltpu
from jax.sharding import PartitionSpec as P

BOX = 256
TILT_STEPS = 32
GRID = 65
CAND = 8
GPAD = 80
BLOCK = 16
ROWS = 16
CHIPS = 8
PIECE = 144
CTF_PHASE = 0.1
MESH = pl.DeviceIdType.MESH
BF16 = jnp.bfloat16
F32 = jnp.float32

GATHER = ((2, 0), (-2, 0), (1, 0), (-1, 0), (1, -2), (-1, 2), (2, -2), (-2, 2))
REDUCE = ((1, 3), (-1, -3), (2, 4), (-2, 4), (1, 1), (-1, -1), (2, 2), (-2, -2))


def first_row(align):
    return align * ROWS


def sin_cos(angle):
    turns = jnp.floor(angle * F32(0.15915494309189535) + F32(0.5))
    half = ((angle - turns * F32(6.28125)) - turns * F32(0.0019353071795864769)) * F32(0.5)
    sq = half * half
    s = F32(-1.0 / 39916800.0)
    for coefficient in (1.0 / 362880.0, -1.0 / 5040.0, 1.0 / 120.0, -1.0 / 6.0, 1.0):
        s = s * sq + F32(coefficient)
    s = s * half
    c = F32(1.0 / 479001600.0)
    for coefficient in (-1.0 / 3628800.0, 1.0 / 40320.0, -1.0 / 720.0, 1.0 / 24.0, -0.5, 1.0):
        c = c * sq + F32(coefficient)
    return F32(2.0) * s * c, F32(1.0) - F32(2.0) * s * s


def tilt_weights(g, plane, ky):
    offset = (g - TILT_STEPS) * (ky - BOX // 2)
    lower = (BOX // 2 + lax.shift_right_arithmetic(offset, 5)) & (BOX - 1)
    upper = (lower + 1) & (BOX - 1)
    fraction = (offset & (TILT_STEPS - 1)).astype(F32) * F32(1.0 / TILT_STEPS)
    zero = jnp.zeros_like(fraction)
    weights = jnp.where(plane == lower, F32(1.0) - fraction, zero) + jnp.where(plane == upper, fraction, zero)
    return jnp.where(g < GRID, weights, zero).astype(BF16)


def iota(shape, axis):
    return lax.broadcasted_iota(jnp.int32, shape, axis)


def dot_nt(a, b):
    return lax.dot_general(a, b, (((1,), (1,)), ((), ())), preferred_element_type=F32)


def dot_nn(a, b):
    return jnp.dot(a, b, preferred_element_type=F32)


def pack(x):
    left, right = x[GRID - 1 :, :128], x[GRID - 1 :, 128:]
    row = iota(left.shape, 0)
    zero = jnp.zeros_like(left)
    last = jnp.where(row == 0, left, jnp.where(row == 1, pltpu.roll(right, 1, 0), zero))
    return jnp.concatenate([x[: GRID - 1, :128], x[: GRID - 1, 128:], last], axis=0)


def unpack(x):
    n = GRID - 1
    last = x[2 * n :]
    top = jnp.concatenate([x[:n], x[n : 2 * n]], axis=1)
    return jnp.concatenate(
        [top, jnp.concatenate([last, pltpu.roll(last, last.shape[0] - 1, 0)], axis=1)], axis=0
    )


def kernel(
    n_slab, n_align, count_ref, orient_hbm, defocus_hbm, vol_hbm, img_ref, bp_ref, post_ref,
    img_buf, lhs, perm, vol_ref, orient_ref, defocus_ref, dcol, volt, planes, sec, dist, energy, pick,
    osum, psend, precv, rsend, rrecv, bsend, brecv,
    img_sem, in_sem, a2a_send, a2a_recv, g_ss, g_rs, pt_ss, pt_rs,
    ps_ss, ps_rs, rp_ss, rp_rs, r_ss, r_rs, b_ss, b_rs,
):
    s = lax.axis_index("slab")
    a = lax.axis_index("align")
    z = lax.div(s, 2)
    k = lax.rem(s, 2)
    slots = lhs.shape[1]
    cols = 2 * BOX

    def slab_of(offset, core):
        return 2 * lax.rem(z + (offset % CHIPS), CHIPS) + core

    partner = (2 * z + 1 - k, a)
    sent = []

    def remote(src, dst, send_sem, recv_sem, device):
        return pltpu.make_async_remote_copy(
            src_ref=src, dst_ref=dst, send_sem=send_sem, recv_sem=recv_sem, device_id=device, device_id_type=MESH
        )

    def send(copy):
        copy.start()
        sent.append(copy)

    vol_copy = pltpu.make_async_copy(vol_hbm, vol_ref, in_sem.at[0])
    vol_copy.start()
    defocus_copy = pltpu.make_async_copy(defocus_hbm, defocus_ref, in_sem.at[2])
    defocus_copy.start()
    barrier = pltpu.get_barrier_semaphore()
    for i in range(1, n_slab):
        pl.semaphore_signal(barrier, inc=1, device_id=(lax.rem(s + i, n_slab), a), device_id_type=MESH)
    for i in range(1, n_align):
        pl.semaphore_signal(barrier, inc=1, device_id=(s, lax.rem(a + i, n_align)), device_id_type=MESH)

    n_chunks = img_sem.shape[0]
    chunk = slots // n_chunks

    def image_copy(i):
        part = pl.ds(i * chunk, chunk)
        return pltpu.make_async_copy(img_ref.at[part], img_buf.at[part], img_sem.at[i])


    def half(h):
        return slice(h * BOX, (h + 1) * BOX)

    r = iota((256, 256), 0)
    c = iota((256, 256), 1)
    swap = (lax.shift_right_logical(r, 4) == (c & 15)) & ((r & 15) == lax.shift_right_logical(c, 4))
    perm[...] = jnp.where(swap, F32(1.0), F32(0.0)).astype(BF16)
    vol_copy.wait()
    for h in range(2):
        turned = dot_nn(perm[...], vol_ref[:, :, half(h)].reshape(256, BOX))
        volt[h] = turned.astype(BF16).reshape(ROWS, 16, BOX)

    pl.semaphore_wait(barrier, n_slab + n_align - 2)

    def plane_copy(h, i):
        to = lax.rem(s + i, n_slab)
        return remote(volt.at[h, to], planes.at[h, s], a2a_send.at[h, i], a2a_recv.at[h, i], (to, a))

    for h in range(2):
        for i in range(1, n_slab):
            send(plane_copy(h, i))
    for i in range(n_chunks):
        image_copy(i).start()
    orient_copy = pltpu.make_async_copy(orient_hbm, orient_ref, in_sem.at[1])
    orient_copy.start()
    for h in range(2):
        planes[h, s] = volt[h, s]

    defocus_copy.wait()
    dcol[...] = lax.dot_general(
        defocus_ref[...].reshape(1, slots), jnp.ones((1, 128), BF16), (((0,), (0,)), ((), ())), preferred_element_type=F32
    )
    kx = (iota((BLOCK, BOX), 1) - BOX // 2).astype(F32)
    kx2 = kx * kx * F32(1.0 / (BOX * BOX))
    ky = ((iota((BLOCK, 128), 1) & (ROWS - 1)) + first_row(a) - BOX // 2).astype(F32)
    ky2 = ky * ky * F32(1.0 / (BOX * BOX))

    def ctf_block(first):
        at = pl.ds(pl.multiple_of(first, BLOCK), BLOCK)
        defocus = dcol[at, :]
        sin_x, cos_x = sin_cos(jnp.concatenate([defocus, defocus], axis=1) * kx2)
        sin_y, cos_y = sin_cos(defocus * ky2 + F32(CTF_PHASE))
        rows = dot_nn(perm[...], img_buf[at].reshape(256, cols))
        total = jnp.zeros((BLOCK, BOX), F32)
        for row in range(ROWS):
            wave = sin_x * cos_y[:, row : row + 1] + cos_x * sin_y[:, row : row + 1]
            real = rows[row * BLOCK : (row + 1) * BLOCK, :BOX]
            imag = rows[row * BLOCK : (row + 1) * BLOCK, BOX:]
            total = total + (real * real + imag * imag)
            lhs[row, at, 0:BOX] = (wave * real).astype(BF16)
            lhs[row, at, BOX:cols] = (wave * imag).astype(BF16)
            lhs[row, at, cols : cols + BOX] = (wave * wave).astype(BF16)
        energy[at, :] = total[:, :128] + total[:, 128:]

    def ctf_chunks(low, high):
        @pl.loop(low, high)
        def _(i):
            image_copy(i).wait()

            @pl.loop(0, chunk // (2 * BLOCK))
            def _(j):
                for u in range(2):
                    ctf_block(i * chunk + (2 * j + u) * BLOCK)

    def gather_copy(kind, h):
        to, owner = GATHER[kind]
        row = slab_of(owner, k)
        return remote(sec.at[row, h], sec.at[row, h], g_ss.at[kind, h], g_rs.at[kind, h], (slab_of(to, k), a))

    def relay_copy(offset, h):
        row = slab_of(offset, k)
        slot = offset % CHIPS
        return remote(sec.at[row, h], sec.at[row, h], pt_ss.at[slot, h], pt_rs.at[slot, h], partner)

    cuts = (0, n_chunks // 2, 7 * n_chunks // 8, n_chunks)
    weights = tilt_weights(iota((GPAD, BOX), 0), iota((GPAD, BOX), 1), first_row(a) + s)
    for h in range(2):
        ctf_chunks(cuts[h], cuts[h + 1])
        for i in range(1, n_slab):
            plane_copy(h, i).wait_recv()
        sec[s, h] = pack(dot_nn(weights, planes[h].reshape(BOX, BOX))).astype(BF16)
        for kind in range(4):
            send(gather_copy(kind, h))
        send(relay_copy(0, h))
    ctf_chunks(cuts[2], cuts[3])

    def operand(row):
        real = unpack(sec[row, 0].astype(F32))
        imag = unpack(sec[row, 1].astype(F32))
        square = (real * real + imag * imag).astype(BF16)
        return jnp.concatenate(
            [(real * F32(-2.0)).astype(BF16), (imag * F32(-2.0)).astype(BF16), square], axis=1
        )

    def score(row):
        return dot_nt(lhs[row], operand(row))

    def row_at(offset, core):
        return 2 * lax.rem(z + CHIPS + offset, CHIPS) + core

    def forward(h):
        gather_copy(0, h).wait_recv()
        send(gather_copy(4, h))
        if h == 0:
            send(gather_copy(6, h))
        send(relay_copy(-2, h))
        gather_copy(1, h).wait_recv()
        send(gather_copy(5, h))
        if h == 1:
            send(gather_copy(7, h))
        send(relay_copy(2, h))

    def add_scores(offsets, core):
        if len(offsets) == 1:
            dist[:, :GPAD] += score(row_at(offsets[0], core))
        else:
            @pl.loop(0, len(offsets) // 2)
            def _(i):
                near = offsets[-1] - i
                dist[:, :GPAD] += score(row_at(near, core)) + score(row_at(-near, core))

    forward(0)
    dist[...] = jnp.zeros_like(dist)
    add_scores([0], k)
    forward(1)
    for h in range(2):
        gather_copy(2, h).wait_recv()
        send(relay_copy(-1, h))
        gather_copy(3, h).wait_recv()
        send(relay_copy(1, h))
    add_scores([-2, -1, 1, 2], k)
    for offset in (0, -2, 2, -1, 1):
        for h in range(2):
            relay_copy(offset, h).wait_recv()
    add_scores([0], 1 - k)
    for h in range(2):
        gather_copy(4, h).wait_recv()
        send(relay_copy(-3, h))
        gather_copy(5, h).wait_recv()
        send(relay_copy(3, h))
        gather_copy(6 + h, h).wait_recv()
        send(relay_copy(4, h))
    add_scores([-2, -1, 1, 2], 1 - k)
    add_scores([-3, 3], k)
    add_scores([4], k)
    for offset in (-3, 3, 4):
        for h in range(2):
            relay_copy(offset, h).wait_recv()
    add_scores([-3, 3], 1 - k)
    add_scores([4], 1 - k)

    orient_copy.wait()
    orient = orient_ref[...]
    full = dist[...] + jnp.sum(energy[...], axis=1, keepdims=True)
    full_t = full.T[:GPAD]
    g_ids = iota((GPAD, slots), 0)
    for n in range(CAND):
        chosen = orient[n : n + 1, :] == g_ids
        pick[a, n : n + 1, :] = jnp.sum(jnp.where(chosen, full_t, F32(0.0)), axis=0, keepdims=True)

    def pick_copy(i):
        to = lax.rem(a + i, n_align)
        return remote(pick.at[a], pick.at[a], ps_ss.at[i], ps_rs.at[i], (s, to))

    for i in range(1, n_align):
        send(pick_copy(i))
    for i in range(1, n_align):
        pick_copy(i).wait_recv()
    picked = pick[0]
    for i in range(1, n_align):
        picked = picked + pick[i]
    scores = picked * F32(-1.0 / BOX)
    e = jnp.exp(scores - jnp.max(scores, axis=0, keepdims=True))
    posterior = e / jnp.sum(e, axis=0, keepdims=True)
    posterior = jnp.where(iota((CAND, slots), 1) < count_ref[0], posterior, F32(0.0))
    post_ref[...] = posterior
    per_grid = jnp.zeros((GPAD, slots), F32)
    for n in range(CAND):
        chosen = orient[n : n + 1, :] == g_ids
        per_grid = per_grid + jnp.where(chosen, posterior[n : n + 1, :], F32(0.0))
    per_grid = per_grid.astype(BF16)

    def pair_copy(offset):
        i = offset % CHIPS
        return remote(psend.at[i], precv.at[i], rp_ss.at[i], rp_rs.at[i], partner)

    def make_partner(offset):
        total = dot_nn(per_grid, lhs[slab_of(offset, 1 - k), :, 0:cols])
        for h in range(2):
            psend[offset % CHIPS, h] = pack(total[:, half(h)]).astype(BF16)
        send(pair_copy(offset))

    def make_own(offset):
        total = dot_nn(per_grid, lhs[slab_of(offset, k), :, 0:cols])
        for h in range(2):
            osum[offset % CHIPS, h] = pack(total[:, half(h)])

    def pair_sum(offset, h):
        return osum[offset % CHIPS, h] + precv[offset % CHIPS, h].astype(F32)

    def reduce_copy(kind, h):
        to = (slab_of(REDUCE[kind][0], k), a)
        return remote(rsend.at[kind, h], rrecv.at[kind, h], r_ss.at[kind, h], r_rs.at[kind, h], to)

    def reduce_send(kind, h, extra=()):
        total = pair_sum(REDUCE[kind][1], h)
        for other in extra:
            reduce_copy(other, h).wait_recv()
            total = total + rrecv[other, h].astype(F32)
        rsend[kind, h] = total.astype(BF16)
        send(reduce_copy(kind, h))

    for offset in (3, -3, 4):
        make_partner(offset)
    for offset in (3, -3, 4):
        make_own(offset)
    for h in range(2):
        for kind in (0, 1, 3 - h):
            if h == 0:
                pair_copy(REDUCE[kind][1]).wait_recv()
            reduce_send(kind, h)
    for offset in (1, -1, 2, -2, 0):
        make_partner(offset)
    for offset in (1, -1, 2, -2):
        make_own(offset)
    for offset in (1, -1, 2, -2):
        pair_copy(offset).wait_recv()

    def back_copy(h, i):
        to = lax.rem(s + i, n_slab)
        return remote(bsend.at[h, to], brecv.at[h, s], b_ss.at[h, i], b_rs.at[h, i], (to, a))

    weights_t = tilt_weights(
        lax.rem(iota((BOX, 2 * GPAD), 1), GPAD), iota((BOX, 2 * GPAD), 0), first_row(a) + s
    )

    def round_two(h):
        reduce_send(4, h)
        reduce_send(5, h)
        reduce_send(6, h, (0, 2) if h == 1 else (0,))
        reduce_send(7, h, (1, 3) if h == 0 else (1,))

    def back_project(h):
        total = pair_sum(0, h)
        for kind in range(4, 8):
            reduce_copy(kind, h).wait_recv()
            total = total + rrecv[kind, h].astype(F32)
        total = unpack(total)
        high = total.astype(BF16)
        low = (total - high.astype(F32)).astype(BF16)
        back = dot_nn(weights_t, jnp.concatenate([high, low], axis=0)).astype(BF16)
        bsend[h] = back.reshape(n_slab, 16, BOX)
        for i in range(1, n_slab):
            send(back_copy(h, i))
        brecv[h, s] = bsend[h, s]

    round_two(0)
    make_own(0)
    round_two(1)
    pair_copy(0).wait_recv()
    back_project(0)
    back_project(1)
    for h in range(2):
        for i in range(1, n_slab):
            back_copy(h, i).wait_recv()
        turned = dot_nn(perm[...], brecv[h].reshape(256, BOX))
        bp_ref[:, :, half(h)] = turned.reshape(16, ROWS, BOX)

    for copy in sent:
        copy.wait_send()


def on_device(n_slab, n_align, volume, images, orient, defocus, particle_counts):
    slots = images.shape[0]
    cols = 2 * BOX
    n_chunks = 8
    dma = pltpu.SemaphoreType.DMA
    vmem = pl.BlockSpec(memory_space=pltpu.VMEM)
    hbm = pl.BlockSpec(memory_space=pltpu.HBM)
    back_projection, posterior = pl.pallas_call(
        functools.partial(kernel, n_slab, n_align),
        out_shape=(
            jax.ShapeDtypeStruct((16, ROWS, cols), F32),
            jax.ShapeDtypeStruct((CAND, slots), F32),
        ),
        in_specs=[pl.BlockSpec(memory_space=pltpu.SMEM), hbm, hbm, hbm, hbm],
        out_specs=(vmem, vmem),
        scratch_shapes=[
            pltpu.VMEM((slots, ROWS, cols), BF16),
            pltpu.VMEM((ROWS, slots, cols + BOX), BF16),
            pltpu.VMEM((256, 256), BF16),
            pltpu.VMEM((16, ROWS, cols), BF16),
            pltpu.VMEM((CAND, slots), jnp.int32),
            pltpu.VMEM((slots,), BF16),
            pltpu.VMEM((slots, 128), F32),
            pltpu.VMEM((2, ROWS, 16, BOX), BF16),
            pltpu.VMEM((2, n_slab, 16, BOX), BF16),
            pltpu.VMEM((ROWS, 2, PIECE, 128), BF16),
            pltpu.VMEM((slots, 128), F32),
            pltpu.VMEM((slots, 128), F32),
            pltpu.VMEM((n_align, CAND, slots), F32),
            pltpu.VMEM((CHIPS, 2, PIECE, 128), F32),
            pltpu.VMEM((CHIPS, 2, PIECE, 128), BF16),
            pltpu.VMEM((CHIPS, 2, PIECE, 128), BF16),
            pltpu.VMEM((8, 2, PIECE, 128), BF16),
            pltpu.VMEM((8, 2, PIECE, 128), BF16),
            pltpu.VMEM((2, n_slab, 16, BOX), BF16),
            pltpu.VMEM((2, n_slab, 16, BOX), BF16),
            dma((n_chunks,)),
            dma((3,)),
            dma((2, n_slab)),
            dma((2, n_slab)),
            dma((8, 2)),
            dma((8, 2)),
            dma((CHIPS, 2)),
            dma((CHIPS, 2)),
            dma((n_align,)),
            dma((n_align,)),
            dma((CHIPS,)),
            dma((CHIPS,)),
            dma((8, 2)),
            dma((8, 2)),
            dma((2, n_slab)),
            dma((2, n_slab)),
        ],
        compiler_params=pltpu.CompilerParams(
            collective_id=0, has_side_effects=True, vmem_limit_bytes=48 * 1024 * 1024
        ),
    )(particle_counts, orient.T, defocus, volume, images)
    return back_projection, posterior.T


def solution(mesh):
    return jax.shard_map(
        functools.partial(on_device, mesh.shape["slab"], mesh.shape["align"]),
        mesh=mesh,
        in_specs=(
            P("slab", "align", None),
            P("slab", "align", None),
            P("slab", None),
            P("slab"),
            P("slab"),
        ),
        out_specs=(P("slab", "align", None), P("slab", None)),
        check_vma=False,
    )
```

```python
import functools

import jax
import jax.numpy as jnp
from jax import lax
from jax.experimental import pallas as pl
from jax.experimental.pallas import tpu as pltpu
from jax.sharding import PartitionSpec as P

BOX = 256
TILT_STEPS = 32
GRID = 65
CAND = 8
GPAD = 80
BLOCK = 16
ROWS = 16
CHIPS = 8
PIECE = 144
CTF_PHASE = 0.1
MESH = pl.DeviceIdType.MESH
BF16 = jnp.bfloat16
F32 = jnp.float32

GATHER = ((2, 0), (-2, 0), (1, 0), (-1, 0), (1, -2), (-1, 2), (2, -2), (-2, 2))
REDUCE = ((1, 3), (-1, -3), (2, 4), (-2, 4), (1, 1), (-1, -1), (2, 2), (-2, -2))


def first_row(align):
    return align * ROWS


def sin_cos(angle):
    turns = jnp.floor(angle * F32(0.15915494309189535) + F32(0.5))
    half = ((angle - turns * F32(6.28125)) - turns * F32(0.0019353071795864769)) * F32(0.5)
    sq = half * half
    s = F32(-1.0 / 39916800.0)
    for coefficient in (1.0 / 362880.0, -1.0 / 5040.0, 1.0 / 120.0, -1.0 / 6.0, 1.0):
        s = s * sq + F32(coefficient)
    s = s * half
    c = F32(1.0 / 479001600.0)
    for coefficient in (-1.0 / 3628800.0, 1.0 / 40320.0, -1.0 / 720.0, 1.0 / 24.0, -0.5, 1.0):
        c = c * sq + F32(coefficient)
    return F32(2.0) * s * c, F32(1.0) - F32(2.0) * s * s


def tilt_weights(g, plane, ky):
    offset = (g - TILT_STEPS) * (ky - BOX // 2)
    lower = (BOX // 2 + lax.shift_right_arithmetic(offset, 5)) & (BOX - 1)
    upper = (lower + 1) & (BOX - 1)
    fraction = (offset & (TILT_STEPS - 1)).astype(F32) * F32(1.0 / TILT_STEPS)
    zero = jnp.zeros_like(fraction)
    weights = jnp.where(plane == lower, F32(1.0) - fraction, zero) + jnp.where(plane == upper, fraction, zero)
    return jnp.where(g < GRID, weights, zero).astype(BF16)


def iota(shape, axis):
    return lax.broadcasted_iota(jnp.int32, shape, axis)


def dot_nt(a, b):
    return lax.dot_general(a, b, (((1,), (1,)), ((), ())), preferred_element_type=F32)


def dot_nn(a, b):
    return jnp.dot(a, b, preferred_element_type=F32)


def pack(x):
    left, right = x[GRID - 1 :, :128], x[GRID - 1 :, 128:]
    row = iota(left.shape, 0)
    zero = jnp.zeros_like(left)
    last = jnp.where(row == 0, left, jnp.where(row == 1, pltpu.roll(right, 1, 0), zero))
    return jnp.concatenate([x[: GRID - 1, :128], x[: GRID - 1, 128:], last], axis=0)


def unpack(x):
    n = GRID - 1
    last = x[2 * n :]
    top = jnp.concatenate([x[:n], x[n : 2 * n]], axis=1)
    return jnp.concatenate(
        [top, jnp.concatenate([last, pltpu.roll(last, last.shape[0] - 1, 0)], axis=1)], axis=0
    )


def swap_matrix():
    r = iota((256, 256), 0)
    c = iota((256, 256), 1)
    swap = (lax.shift_right_logical(r, 4) == (c & 15)) & ((r & 15) == lax.shift_right_logical(c, 4))
    return jnp.where(swap, F32(1.0), F32(0.0)).astype(BF16)


def turn(planes_hbm, posterior_hbm, bp_hbm, post_hbm, planes_ref, bp_ref, sems):
    def copy_in(h):
        return pltpu.make_async_copy(planes_hbm.at[h], planes_ref.at[h], sems.at[h])

    def copy_out(h):
        part = pl.ds(h * BOX, BOX)
        return pltpu.make_async_copy(bp_ref.at[:, :, part], bp_hbm.at[:, :, part], sems.at[2 + h])

    post_copy = pltpu.make_async_copy(posterior_hbm, post_hbm, sems.at[4])
    copy_in(0).start()
    copy_in(1).start()
    post_copy.start()
    swap = swap_matrix()
    for h in range(2):
        copy_in(h).wait()
        turned = dot_nn(swap, planes_ref[h].reshape(256, BOX))
        bp_ref[:, :, h * BOX : (h + 1) * BOX] = turned.reshape(16, ROWS, BOX)
        copy_out(h).start()
    for h in range(2):
        copy_out(h).wait()
    post_copy.wait()


def kernel(
    n_slab, n_align, count_ref, orient_hbm, defocus_hbm, vol_hbm, img_ref, brecv, post_hbm,
    img_buf, lhs, perm, vol_ref, orient_ref, defocus_ref, dcol, volt, planes, sec, dist, energy, pick,
    osum, psend, precv, rsend, rrecv, bsend, post_ref,
    img_sem, in_sem, a2a_send, a2a_recv, g_ss, g_rs, pt_ss, pt_rs,
    ps_ss, ps_rs, rp_ss, rp_rs, r_ss, r_rs, b_ss, b_rs,
):
    s = lax.axis_index("slab")
    a = lax.axis_index("align")
    z = lax.shift_right_logical(s, 1)
    k = s & 1
    slots = lhs.shape[1]
    cols = 2 * BOX

    def slab_of(offset, core):
        return 2 * ((z + offset % CHIPS) & (CHIPS - 1)) + core

    partner = (2 * z + 1 - k, a)
    sent = []

    def remote(src, dst, send_sem, recv_sem, device):
        return pltpu.make_async_remote_copy(
            src_ref=src, dst_ref=dst, send_sem=send_sem, recv_sem=recv_sem, device_id=device, device_id_type=MESH
        )

    def send(copy):
        copy.start()
        sent.append(copy)

    def drain():
        for copy in sent:
            copy.wait_send()
        sent.clear()

    vol_copy = pltpu.make_async_copy(vol_hbm, vol_ref, in_sem.at[0])
    vol_copy.start()
    defocus_copy = pltpu.make_async_copy(defocus_hbm, defocus_ref, in_sem.at[2])
    defocus_copy.start()
    barrier = pltpu.get_barrier_semaphore()
    for i in range(1, n_slab):
        pl.semaphore_signal(barrier, inc=1, device_id=((s + i) & (n_slab - 1), a), device_id_type=MESH)
    for i in range(1, n_align):
        pl.semaphore_signal(barrier, inc=1, device_id=(s, (a + i) & (n_align - 1)), device_id_type=MESH)

    n_chunks = img_sem.shape[0]
    chunk = slots // n_chunks

    def image_copy(i):
        part = pl.ds(i * chunk, chunk)
        return pltpu.make_async_copy(img_ref.at[part], img_buf.at[part], img_sem.at[i])


    def half(h):
        return slice(h * BOX, (h + 1) * BOX)

    perm[...] = swap_matrix()
    vol_copy.wait()
    for h in range(2):
        turned = dot_nn(perm[...], vol_ref[:, :, half(h)].reshape(256, BOX))
        volt[h] = turned.astype(BF16).reshape(ROWS, 16, BOX)

    pl.semaphore_wait(barrier, n_slab + n_align - 2)

    def plane_copy(h, i):
        to = (s + i) & (n_slab - 1)
        return remote(volt.at[h, to], planes.at[h, s], a2a_send.at[h], a2a_recv.at[h], (to, a))

    def all_planes(h):
        peers = pl.ds(0, n_slab - 1)
        return remote(volt.at[h, peers], planes.at[h, peers], a2a_send.at[h], a2a_recv.at[h], partner)

    for h in range(2):
        for i in range(1, n_slab):
            plane_copy(h, i).start()
    for i in range(n_chunks):
        image_copy(i).start()
    orient_copy = pltpu.make_async_copy(orient_hbm, orient_ref, in_sem.at[1])
    orient_copy.start()
    for h in range(2):
        planes[h, s] = volt[h, s]

    defocus_copy.wait()
    dcol[...] = lax.dot_general(
        defocus_ref[...].reshape(1, slots), jnp.ones((1, 128), BF16), (((0,), (0,)), ((), ())), preferred_element_type=F32
    )
    kx = (iota((BLOCK, BOX), 1) - BOX // 2).astype(F32)
    kx2 = kx * kx * F32(1.0 / (BOX * BOX))
    ky = ((iota((BLOCK, 128), 1) & (ROWS - 1)) + first_row(a) - BOX // 2).astype(F32)
    ky2 = ky * ky * F32(1.0 / (BOX * BOX))

    def ctf_block(first):
        at = pl.ds(pl.multiple_of(first, BLOCK), BLOCK)
        defocus = dcol[at, :]
        sin_x, cos_x = sin_cos(jnp.concatenate([defocus, defocus], axis=1) * kx2)
        sin_y, cos_y = sin_cos(defocus * ky2 + F32(CTF_PHASE))
        rows = dot_nn(perm[...], img_buf[at].reshape(256, cols))
        total = jnp.zeros((BLOCK, BOX), F32)
        for row in range(ROWS):
            wave = sin_x * cos_y[:, row : row + 1] + cos_x * sin_y[:, row : row + 1]
            real = rows[row * BLOCK : (row + 1) * BLOCK, :BOX]
            imag = rows[row * BLOCK : (row + 1) * BLOCK, BOX:]
            total = total + (real * real + imag * imag)
            lhs[row, at, 0:BOX] = (wave * real).astype(BF16)
            lhs[row, at, BOX:cols] = (wave * imag).astype(BF16)
            lhs[row, at, cols : cols + BOX] = (wave * wave).astype(BF16)
        energy[at, :] = total[:, :128] + total[:, 128:]

    def ctf_chunks(low, high):
        @pl.loop(low, high)
        def _(i):
            image_copy(i).wait()

            @pl.loop(0, chunk // (2 * BLOCK))
            def _(j):
                for u in range(2):
                    ctf_block(i * chunk + (2 * j + u) * BLOCK)

    def gather_copy(kind, h):
        to, owner = GATHER[kind]
        row = slab_of(owner, k)
        return remote(sec.at[row, h], sec.at[row, h], g_ss.at[kind, h], g_rs.at[kind, h], (slab_of(to, k), a))

    def relay_copy(offset, h):
        row = slab_of(offset, k)
        slot = offset % CHIPS
        return remote(sec.at[row, h], sec.at[row, h], pt_ss.at[slot, h], pt_rs.at[slot, h], partner)

    cuts = (0, n_chunks // 2, 7 * n_chunks // 8, n_chunks)
    weights = tilt_weights(iota((GPAD, BOX), 0), iota((GPAD, BOX), 1), first_row(a) + s)
    for h in range(2):
        ctf_chunks(cuts[h], cuts[h + 1])
        all_planes(h).wait_recv()
        sec[s, h] = pack(dot_nn(weights, planes[h].reshape(BOX, BOX))).astype(BF16)
        for kind in range(4):
            send(gather_copy(kind, h))
        send(relay_copy(0, h))
    ctf_chunks(cuts[2], cuts[3])

    def operand(row):
        real = unpack(sec[row, 0].astype(F32))
        imag = unpack(sec[row, 1].astype(F32))
        square = (real * real + imag * imag).astype(BF16)
        return jnp.concatenate(
            [(real * F32(-2.0)).astype(BF16), (imag * F32(-2.0)).astype(BF16), square], axis=1
        )

    def score(row):
        return dot_nt(lhs[row], operand(row))

    def row_at(offset, core):
        return 2 * ((z + CHIPS + offset) & (CHIPS - 1)) + core

    def forward(h):
        gather_copy(0, h).wait_recv()
        send(gather_copy(4, h))
        if h == 0:
            send(gather_copy(6, h))
        send(relay_copy(-2, h))
        gather_copy(1, h).wait_recv()
        send(gather_copy(5, h))
        if h == 1:
            send(gather_copy(7, h))
        send(relay_copy(2, h))

    def add_scores(offsets, core):
        if len(offsets) == 1:
            dist[:, :GPAD] += score(row_at(offsets[0], core))
        else:
            @pl.loop(0, len(offsets) // 2)
            def _(i):
                near = offsets[-1] - i
                dist[:, :GPAD] += score(row_at(near, core)) + score(row_at(-near, core))

    forward(0)
    dist[...] = jnp.zeros_like(dist) + jnp.sum(energy[...], axis=1, keepdims=True)
    add_scores([0], k)
    forward(1)
    for h in range(2):
        gather_copy(2, h).wait_recv()
        send(relay_copy(-1, h))
        gather_copy(3, h).wait_recv()
        send(relay_copy(1, h))
    add_scores([-2, -1, 1, 2], k)
    for offset in (0, -2, 2, -1, 1):
        for h in range(2):
            relay_copy(offset, h).wait_recv()
    add_scores([0], 1 - k)
    for h in range(2):
        gather_copy(4, h).wait_recv()
        send(relay_copy(-3, h))
        gather_copy(5, h).wait_recv()
        send(relay_copy(3, h))
        gather_copy(6 + h, h).wait_recv()
        send(relay_copy(4, h))
    add_scores([-2, -1, 1, 2], 1 - k)
    add_scores([-3, 3], k)
    add_scores([4], k)
    for offset in (-3, 3, 4):
        for h in range(2):
            relay_copy(offset, h).wait_recv()
    add_scores([-3, 3], 1 - k)
    add_scores([4], 1 - k)

    orient_copy.wait()
    orient = orient_ref[...]
    full_t = dist[...].T[:GPAD]
    g_ids = iota((GPAD, slots), 0)
    for n in range(CAND):
        chosen = orient[n : n + 1, :] == g_ids
        pick[a, n : n + 1, :] = jnp.sum(jnp.where(chosen, full_t, F32(0.0)), axis=0, keepdims=True)

    def pick_copy(i):
        to = (a + i) & (n_align - 1)
        return remote(pick.at[a], pick.at[a], ps_ss.at[0], ps_rs.at[0], (s, to))

    def all_picks():
        peers = pl.ds(0, n_align - 1)
        return remote(pick.at[peers], pick.at[peers], ps_ss.at[0], ps_rs.at[0], partner)

    for i in range(1, n_align):
        pick_copy(i).start()
    for h in range(2):
        all_planes(h).wait_send()
    drain()
    if n_align > 1:
        all_picks().wait_recv()
        all_picks().wait_send()
    picked = pick[0]
    for i in range(1, n_align):
        picked = picked + pick[i]
    scores = picked * F32(-1.0 / BOX)
    e = jnp.exp(scores - jnp.max(scores, axis=0, keepdims=True))
    posterior = e / jnp.sum(e, axis=0, keepdims=True)
    posterior = jnp.where(iota((CAND, slots), 1) < count_ref[0], posterior, F32(0.0))
    post_ref[...] = posterior
    post_copy = pltpu.make_async_copy(post_ref, post_hbm, in_sem.at[3])
    post_copy.start()
    per_grid = jnp.zeros((GPAD, slots), F32)
    for n in range(CAND):
        chosen = orient[n : n + 1, :] == g_ids
        per_grid = per_grid + jnp.where(chosen, posterior[n : n + 1, :], F32(0.0))
    per_grid = per_grid.astype(BF16)

    def pair_copy(offset):
        i = offset % CHIPS
        return remote(psend.at[i], precv.at[i], rp_ss.at[i], rp_rs.at[i], partner)

    def make_partner(offset):
        total = dot_nn(per_grid, lhs[slab_of(offset, 1 - k), :, 0:cols])
        for h in range(2):
            psend[offset % CHIPS, h] = pack(total[:, half(h)]).astype(BF16)
        send(pair_copy(offset))

    def make_own(offset):
        total = dot_nn(per_grid, lhs[slab_of(offset, k), :, 0:cols])
        for h in range(2):
            osum[offset % CHIPS, h] = pack(total[:, half(h)])

    def pair_sum(offset, h):
        return osum[offset % CHIPS, h] + precv[offset % CHIPS, h].astype(F32)

    def reduce_copy(kind, h):
        to = (slab_of(REDUCE[kind][0], k), a)
        return remote(rsend.at[kind, h], rrecv.at[kind, h], r_ss.at[kind, h], r_rs.at[kind, h], to)

    def reduce_send(kind, h, extra=()):
        total = pair_sum(REDUCE[kind][1], h)
        for other in extra:
            reduce_copy(other, h).wait_recv()
            total = total + rrecv[other, h].astype(F32)
        rsend[kind, h] = total.astype(BF16)
        send(reduce_copy(kind, h))

    make_partner(3)
    make_partner(-3)
    make_own(3)
    make_own(-3)
    make_partner(4)
    for kind in (0, 1):
        pair_copy(REDUCE[kind][1]).wait_recv()
        reduce_send(kind, 0)
    make_own(4)
    for kind in (0, 1):
        reduce_send(kind, 1)
    make_partner(1)
    make_partner(-1)
    pair_copy(4).wait_recv()
    reduce_send(3, 0)
    reduce_send(2, 1)
    for offset in (2, -2, 0):
        make_partner(offset)
    for offset in (1, -1, 2, -2):
        make_own(offset)
    for offset in (1, -1, 2, -2):
        pair_copy(offset).wait_recv()

    def back_copy(h, i):
        to = (s + i) & (n_slab - 1)
        return remote(bsend.at[h, to], brecv.at[h, s], b_ss.at[h], b_rs.at[h], (to, a))

    weights_t = tilt_weights(
        lax.rem(iota((BOX, 2 * GPAD), 1), GPAD), iota((BOX, 2 * GPAD), 0), first_row(a) + s
    )

    def all_back(h):
        peers = pl.ds(0, n_slab - 1)
        return remote(bsend.at[h, peers], brecv.at[h, peers], b_ss.at[h], b_rs.at[h], partner)

    def own_copy(h):
        return pltpu.make_async_copy(bsend.at[h, s], brecv.at[h, s], img_sem.at[h])

    def round_two(h):
        reduce_send(4, h)
        reduce_send(5, h)
        reduce_send(6, h, (0, 2) if h == 1 else (0,))
        reduce_send(7, h, (1, 3) if h == 0 else (1,))

    def back_project(h):
        total = pair_sum(0, h)
        for kind in range(4, 8):
            reduce_copy(kind, h).wait_recv()
            total = total + rrecv[kind, h].astype(F32)
        total = unpack(total)
        high = total.astype(BF16)
        low = (total - high.astype(F32)).astype(BF16)
        back = dot_nn(weights_t, jnp.concatenate([high, low], axis=0)).astype(BF16)
        bsend[h] = back.reshape(n_slab, 16, BOX)
        for i in range(1, n_slab):
            back_copy(h, i).start()
        own_copy(h).start()

    round_two(0)
    make_own(0)
    round_two(1)
    pair_copy(0).wait_recv()
    back_project(0)
    back_project(1)
    post_copy.wait()
    drain()
    for h in range(2):
        own_copy(h).wait()
        all_back(h).wait_send()
        all_back(h).wait_recv()


def on_device(n_slab, n_align, volume, images, orient, defocus, particle_counts):
    slots = images.shape[0]
    cols = 2 * BOX
    n_chunks = 8
    dma = pltpu.SemaphoreType.DMA
    hbm = pl.BlockSpec(memory_space=pltpu.HBM)
    planes, posterior = pl.pallas_call(
        functools.partial(kernel, n_slab, n_align),
        out_shape=(
            jax.ShapeDtypeStruct((2, n_slab, 16, BOX), BF16),
            jax.ShapeDtypeStruct((CAND, slots), F32),
        ),
        in_specs=[pl.BlockSpec(memory_space=pltpu.SMEM), hbm, hbm, hbm, hbm],
        out_specs=(hbm, hbm),
        scratch_shapes=[
            pltpu.VMEM((slots, ROWS, cols), BF16),
            pltpu.VMEM((ROWS, slots, cols + BOX), BF16),
            pltpu.VMEM((256, 256), BF16),
            pltpu.VMEM((16, ROWS, cols), BF16),
            pltpu.VMEM((CAND, slots), jnp.int32),
            pltpu.VMEM((slots,), BF16),
            pltpu.VMEM((slots, 128), F32),
            pltpu.VMEM((2, ROWS, 16, BOX), BF16),
            pltpu.VMEM((2, n_slab, 16, BOX), BF16),
            pltpu.VMEM((ROWS, 2, PIECE, 128), BF16),
            pltpu.VMEM((slots, 128), F32),
            pltpu.VMEM((slots, 128), F32),
            pltpu.VMEM((n_align, CAND, slots), F32),
            pltpu.VMEM((CHIPS, 2, PIECE, 128), F32),
            pltpu.VMEM((CHIPS, 2, PIECE, 128), BF16),
            pltpu.VMEM((CHIPS, 2, PIECE, 128), BF16),
            pltpu.VMEM((8, 2, PIECE, 128), BF16),
            pltpu.VMEM((8, 2, PIECE, 128), BF16),
            pltpu.VMEM((2, n_slab, 16, BOX), BF16),
            pltpu.VMEM((CAND, slots), F32),
            dma((n_chunks,)),
            dma((5,)),
            dma((2,)),
            dma((2,)),
            dma((8, 2)),
            dma((8, 2)),
            dma((CHIPS, 2)),
            dma((CHIPS, 2)),
            dma((1,)),
            dma((1,)),
            dma((CHIPS,)),
            dma((CHIPS,)),
            dma((8, 2)),
            dma((8, 2)),
            dma((2,)),
            dma((2,)),
        ],
        compiler_params=pltpu.CompilerParams(
            collective_id=0, has_side_effects=True, vmem_limit_bytes=60 * 1024 * 1024
        ),
    )(particle_counts, orient.T, defocus, volume, images)
    back_projection, posterior = pl.pallas_call(
        turn,
        out_shape=(
            jax.ShapeDtypeStruct((16, ROWS, cols), F32),
            jax.ShapeDtypeStruct((CAND, slots), F32),
        ),
        in_specs=[hbm, hbm],
        out_specs=(hbm, hbm),
        scratch_shapes=[
            pltpu.VMEM((2, n_slab, 16, BOX), BF16),
            pltpu.VMEM((16, ROWS, cols), F32),
            dma((5,)),
        ],
        compiler_params=pltpu.CompilerParams(vmem_limit_bytes=60 * 1024 * 1024),
    )(planes, posterior)
    return back_projection, posterior.T


def solution(mesh):
    return jax.shard_map(
        functools.partial(on_device, mesh.shape["slab"], mesh.shape["align"]),
        mesh=mesh,
        in_specs=(
            P("slab", "align", None),
            P("slab", "align", None),
            P("slab", None),
            P("slab"),
            P("slab"),
        ),
        out_specs=(P("slab", "align", None), P("slab", None)),
        check_vma=False,
    )
```

```python
import functools

import jax
import jax.numpy as jnp
from jax import lax
from jax.experimental import pallas as pl
from jax.experimental.pallas import tpu as pltpu
from jax.sharding import PartitionSpec as P

BOX = 256
TILT_STEPS = 32
GRID = 65
CAND = 8
GPAD = 80
BLOCK = 16
ROWS = 16
CHIPS = 8
PIECE = 144
CTF_PHASE = 0.1
MESH = pl.DeviceIdType.MESH
BF16 = jnp.bfloat16
F32 = jnp.float32

GATHER = ((2, 0), (-2, 0), (1, 0), (-1, 0), (1, -2), (-1, 2), (2, -2), (-2, 2))
REDUCE = ((1, 3), (-1, -3), (2, 4), (-2, 4), (1, 1), (-1, -1), (2, 2), (-2, -2))


def first_row(align):
    return align * ROWS


def sin_cos(angle):
    turns = jnp.floor(angle * F32(0.15915494309189535) + F32(0.5))
    half = ((angle - turns * F32(6.28125)) - turns * F32(0.0019353071795864769)) * F32(0.5)
    sq = half * half
    s = F32(-1.0 / 39916800.0)
    for coefficient in (1.0 / 362880.0, -1.0 / 5040.0, 1.0 / 120.0, -1.0 / 6.0, 1.0):
        s = s * sq + F32(coefficient)
    s = s * half
    c = F32(1.0 / 479001600.0)
    for coefficient in (-1.0 / 3628800.0, 1.0 / 40320.0, -1.0 / 720.0, 1.0 / 24.0, -0.5, 1.0):
        c = c * sq + F32(coefficient)
    return F32(2.0) * s * c, F32(1.0) - F32(2.0) * s * s


def tilt_weights(g, plane, ky):
    offset = (g - TILT_STEPS) * (ky - BOX // 2)
    lower = (BOX // 2 + lax.shift_right_arithmetic(offset, 5)) & (BOX - 1)
    upper = (lower + 1) & (BOX - 1)
    fraction = (offset & (TILT_STEPS - 1)).astype(F32) * F32(1.0 / TILT_STEPS)
    zero = jnp.zeros_like(fraction)
    weights = jnp.where(plane == lower, F32(1.0) - fraction, zero) + jnp.where(plane == upper, fraction, zero)
    return jnp.where(g < GRID, weights, zero).astype(BF16)


def iota(shape, axis):
    return lax.broadcasted_iota(jnp.int32, shape, axis)


def dot_nt(a, b):
    return lax.dot_general(a, b, (((1,), (1,)), ((), ())), preferred_element_type=F32)


def dot_nn(a, b):
    return jnp.dot(a, b, preferred_element_type=F32)


def pack(x):
    left, right = x[GRID - 1 :, :128], x[GRID - 1 :, 128:]
    row = iota(left.shape, 0)
    zero = jnp.zeros_like(left)
    last = jnp.where(row == 0, left, jnp.where(row == 1, pltpu.roll(right, 1, 0), zero))
    return jnp.concatenate([x[: GRID - 1, :128], x[: GRID - 1, 128:], last], axis=0)


def unpack(x):
    n = GRID - 1
    last = x[2 * n :]
    top = jnp.concatenate([x[:n], x[n : 2 * n]], axis=1)
    return jnp.concatenate(
        [top, jnp.concatenate([last, pltpu.roll(last, last.shape[0] - 1, 0)], axis=1)], axis=0
    )


def swap_matrix():
    r = iota((256, 256), 0)
    c = iota((256, 256), 1)
    swap = (lax.shift_right_logical(r, 4) == (c & 15)) & ((r & 15) == lax.shift_right_logical(c, 4))
    return jnp.where(swap, F32(1.0), F32(0.0)).astype(BF16)


def turn(planes_hbm, posterior_hbm, bp_hbm, post_hbm, planes_ref, bp_ref, sems):
    def copy_in(h):
        return pltpu.make_async_copy(planes_hbm.at[h], planes_ref.at[h], sems.at[h])

    def copy_out(h):
        part = pl.ds(h * BOX, BOX)
        return pltpu.make_async_copy(bp_ref.at[:, :, part], bp_hbm.at[:, :, part], sems.at[2 + h])

    post_copy = pltpu.make_async_copy(posterior_hbm, post_hbm, sems.at[4])
    copy_in(0).start()
    copy_in(1).start()
    post_copy.start()
    swap = swap_matrix()
    for h in range(2):
        copy_in(h).wait()
        turned = dot_nn(swap, planes_ref[h].reshape(256, BOX))
        bp_ref[:, :, h * BOX : (h + 1) * BOX] = turned.reshape(16, ROWS, BOX)
        copy_out(h).start()
    for h in range(2):
        copy_out(h).wait()
    post_copy.wait()


def kernel(
    n_slab, n_align, count_ref, orient_hbm, defocus_hbm, vol_hbm, img_ref, brecv, post_hbm,
    img_buf, lhs, perm, vol_ref, orient_ref, defocus_ref, dcol, volt, planes, sec, dist, energy, pick,
    osum, psend, precv, rsend, rrecv, bsend, post_ref,
    img_sem, in_sem, a2a_send, a2a_recv, g_ss, g_rs, pt_ss, pt_rs,
    ps_ss, ps_rs, rp_ss, rp_rs, r_ss, r_rs, b_ss, b_rs,
):
    s = lax.axis_index("slab")
    a = lax.axis_index("align")
    z = lax.shift_right_logical(s, 1)
    k = s & 1
    slots = lhs.shape[1]
    cols = 2 * BOX

    def slab_of(offset, core):
        return 2 * ((z + offset % CHIPS) & (CHIPS - 1)) + core

    partner = (2 * z + 1 - k, a)
    sent = []
    far_first = sorted(range(1, n_slab), key=lambda i: -min(i, n_slab - i))

    def remote(src, dst, send_sem, recv_sem, device):
        return pltpu.make_async_remote_copy(
            src_ref=src, dst_ref=dst, send_sem=send_sem, recv_sem=recv_sem, device_id=device, device_id_type=MESH
        )

    def send(copy):
        copy.start()
        sent.append(copy)

    def drain():
        for copy in sent:
            copy.wait_send()
        sent.clear()

    vol_copy = pltpu.make_async_copy(vol_hbm, vol_ref, in_sem.at[0])
    vol_copy.start()
    defocus_copy = pltpu.make_async_copy(defocus_hbm, defocus_ref, in_sem.at[2])
    defocus_copy.start()
    barrier = pltpu.get_barrier_semaphore()
    for i in range(1, n_slab):
        pl.semaphore_signal(barrier, inc=1, device_id=((s + i) & (n_slab - 1), a), device_id_type=MESH)
    for i in range(1, n_align):
        pl.semaphore_signal(barrier, inc=1, device_id=(s, (a + i) & (n_align - 1)), device_id_type=MESH)

    n_chunks = img_sem.shape[0]
    chunk = slots // n_chunks

    def image_copy(i):
        part = pl.ds(i * chunk, chunk)
        return pltpu.make_async_copy(img_ref.at[part], img_buf.at[part], img_sem.at[i])


    def half(h):
        return slice(h * BOX, (h + 1) * BOX)

    perm[...] = swap_matrix()
    vol_copy.wait()
    for h in range(2):
        turned = dot_nn(perm[...], vol_ref[:, :, half(h)].reshape(256, BOX))
        volt[h] = turned.astype(BF16).reshape(ROWS, 16, BOX)

    pl.semaphore_wait(barrier, n_slab + n_align - 2)

    def plane_copy(h, i):
        to = (s + i) & (n_slab - 1)
        return remote(volt.at[h, to], planes.at[h, s], a2a_send.at[h], a2a_recv.at[h], (to, a))

    def all_planes(h):
        peers = pl.ds(0, n_slab - 1)
        return remote(volt.at[h, peers], planes.at[h, peers], a2a_send.at[h], a2a_recv.at[h], partner)

    for h in range(2):
        for i in far_first:
            plane_copy(h, i).start()
    for i in range(n_chunks):
        image_copy(i).start()
    orient_copy = pltpu.make_async_copy(orient_hbm, orient_ref, in_sem.at[1])
    orient_copy.start()
    for h in range(2):
        planes[h, s] = volt[h, s]

    defocus_copy.wait()
    dcol[...] = lax.dot_general(
        defocus_ref[...].reshape(1, slots), jnp.ones((1, 128), BF16), (((0,), (0,)), ((), ())), preferred_element_type=F32
    )
    kx = (iota((BLOCK, BOX), 1) - BOX // 2).astype(F32)
    kx2 = kx * kx * F32(1.0 / (BOX * BOX))
    ky = ((iota((BLOCK, 128), 1) & (ROWS - 1)) + first_row(a) - BOX // 2).astype(F32)
    ky2 = ky * ky * F32(1.0 / (BOX * BOX))

    def ctf_block(first):
        at = pl.ds(pl.multiple_of(first, BLOCK), BLOCK)
        defocus = dcol[at, :]
        sin_x, cos_x = sin_cos(jnp.concatenate([defocus, defocus], axis=1) * kx2)
        sin_y, cos_y = sin_cos(defocus * ky2 + F32(CTF_PHASE))
        rows = dot_nn(perm[...], img_buf[at].reshape(256, cols))
        total = jnp.zeros((BLOCK, BOX), F32)
        for row in range(ROWS):
            wave = sin_x * cos_y[:, row : row + 1] + cos_x * sin_y[:, row : row + 1]
            real = rows[row * BLOCK : (row + 1) * BLOCK, :BOX]
            imag = rows[row * BLOCK : (row + 1) * BLOCK, BOX:]
            total = total + (real * real + imag * imag)
            lhs[row, at, 0:BOX] = (wave * real).astype(BF16)
            lhs[row, at, BOX:cols] = (wave * imag).astype(BF16)
            lhs[row, at, cols : cols + BOX] = (wave * wave).astype(BF16)
        energy[at, :] = total[:, :128] + total[:, 128:]

    def ctf_chunks(low, high):
        @pl.loop(low, high)
        def _(i):
            image_copy(i).wait()

            @pl.loop(0, chunk // (2 * BLOCK))
            def _(j):
                for u in range(2):
                    ctf_block(i * chunk + (2 * j + u) * BLOCK)

    def gather_copy(kind, h):
        to, owner = GATHER[kind]
        row = slab_of(owner, k)
        return remote(sec.at[row, h], sec.at[row, h], g_ss.at[kind, h], g_rs.at[kind, h], (slab_of(to, k), a))

    def relay_copy(offset, h):
        row = slab_of(offset, k)
        slot = offset % CHIPS
        return remote(sec.at[row, h], sec.at[row, h], pt_ss.at[slot, h], pt_rs.at[slot, h], partner)

    cuts = (0, n_chunks // 2, 7 * n_chunks // 8, n_chunks)
    weights = tilt_weights(iota((GPAD, BOX), 0), iota((GPAD, BOX), 1), first_row(a) + s)
    for h in range(2):
        ctf_chunks(cuts[h], cuts[h + 1])
        all_planes(h).wait_recv()
        sec[s, h] = pack(dot_nn(weights, planes[h].reshape(BOX, BOX))).astype(BF16)
        for kind in range(4):
            send(gather_copy(kind, h))
        send(relay_copy(0, h))
    ctf_chunks(cuts[2], cuts[3])

    def operand(row):
        real = unpack(sec[row, 0].astype(F32))
        imag = unpack(sec[row, 1].astype(F32))
        square = (real * real + imag * imag).astype(BF16)
        return jnp.concatenate(
            [(real * F32(-2.0)).astype(BF16), (imag * F32(-2.0)).astype(BF16), square], axis=1
        )

    def score(row):
        return dot_nt(lhs[row], operand(row))

    def row_at(offset, core):
        return 2 * ((z + CHIPS + offset) & (CHIPS - 1)) + core

    def forward(h):
        gather_copy(0, h).wait_recv()
        send(gather_copy(4, h))
        if h == 0:
            send(gather_copy(6, h))
        send(relay_copy(-2, h))
        gather_copy(1, h).wait_recv()
        send(gather_copy(5, h))
        if h == 1:
            send(gather_copy(7, h))
        send(relay_copy(2, h))

    def add_scores(offsets, core):
        if len(offsets) == 1:
            dist[:, :GPAD] += score(row_at(offsets[0], core))
        else:
            @pl.loop(0, len(offsets) // 2)
            def _(i):
                near = offsets[-1] - i
                dist[:, :GPAD] += score(row_at(near, core)) + score(row_at(-near, core))

    forward(0)
    dist[...] = jnp.zeros_like(dist) + jnp.sum(energy[...], axis=1, keepdims=True)
    add_scores([0], k)
    forward(1)
    for h in range(2):
        gather_copy(2, h).wait_recv()
        send(relay_copy(-1, h))
        gather_copy(3, h).wait_recv()
        send(relay_copy(1, h))
    add_scores([-2, -1, 1, 2], k)
    for offset in (0, -2, 2, -1, 1):
        for h in range(2):
            relay_copy(offset, h).wait_recv()
    add_scores([0], 1 - k)
    for h in range(2):
        gather_copy(4, h).wait_recv()
        send(relay_copy(-3, h))
        gather_copy(5, h).wait_recv()
        send(relay_copy(3, h))
        gather_copy(6 + h, h).wait_recv()
        send(relay_copy(4, h))
    add_scores([-2, -1, 1, 2], 1 - k)
    add_scores([-3, 3], k)
    add_scores([4], k)
    for offset in (-3, 3, 4):
        for h in range(2):
            relay_copy(offset, h).wait_recv()
    add_scores([-3, 3], 1 - k)
    add_scores([4], 1 - k)

    orient_copy.wait()
    orient = orient_ref[...]
    full_t = dist[...].T[:GPAD]
    g_ids = iota((GPAD, slots), 0)
    for n in range(CAND):
        chosen = orient[n : n + 1, :] == g_ids
        pick[a, n : n + 1, :] = jnp.sum(jnp.where(chosen, full_t, F32(0.0)), axis=0, keepdims=True)

    def pick_copy(i):
        to = (a + i) & (n_align - 1)
        return remote(pick.at[a], pick.at[a], ps_ss.at[0], ps_rs.at[0], (s, to))

    def all_picks():
        peers = pl.ds(0, n_align - 1)
        return remote(pick.at[peers], pick.at[peers], ps_ss.at[0], ps_rs.at[0], partner)

    for i in range(1, n_align):
        pick_copy(i).start()
    for h in range(2):
        all_planes(h).wait_send()
    drain()
    if n_align > 1:
        all_picks().wait_recv()
        all_picks().wait_send()
    picked = pick[0]
    for i in range(1, n_align):
        picked = picked + pick[i]
    scores = picked * F32(-1.0 / BOX)
    e = jnp.exp(scores - jnp.max(scores, axis=0, keepdims=True))
    posterior = e / jnp.sum(e, axis=0, keepdims=True)
    posterior = jnp.where(iota((CAND, slots), 1) < count_ref[0], posterior, F32(0.0))
    post_ref[...] = posterior
    post_copy = pltpu.make_async_copy(post_ref, post_hbm, in_sem.at[3])
    post_copy.start()
    per_grid = jnp.zeros((GPAD, slots), F32)
    for n in range(CAND):
        chosen = orient[n : n + 1, :] == g_ids
        per_grid = per_grid + jnp.where(chosen, posterior[n : n + 1, :], F32(0.0))
    per_grid = per_grid.astype(BF16)

    def pair_copy(offset):
        i = offset % CHIPS
        return remote(psend.at[i], precv.at[i], rp_ss.at[i], rp_rs.at[i], partner)

    def make_partner(offset):
        total = dot_nn(per_grid, lhs[slab_of(offset, 1 - k), :, 0:cols])
        for h in range(2):
            psend[offset % CHIPS, h] = pack(total[:, half(h)]).astype(BF16)
        send(pair_copy(offset))

    def make_own(offset):
        total = dot_nn(per_grid, lhs[slab_of(offset, k), :, 0:cols])
        for h in range(2):
            osum[offset % CHIPS, h] = pack(total[:, half(h)])

    def pair_sum(offset, h):
        return osum[offset % CHIPS, h] + precv[offset % CHIPS, h].astype(F32)

    def reduce_copy(kind, h):
        to = (slab_of(REDUCE[kind][0], k), a)
        return remote(rsend.at[kind, h], rrecv.at[kind, h], r_ss.at[kind, h], r_rs.at[kind, h], to)

    def reduce_send(kind, h, extra=()):
        total = pair_sum(REDUCE[kind][1], h)
        for other in extra:
            reduce_copy(other, h).wait_recv()
            total = total + rrecv[other, h].astype(F32)
        rsend[kind, h] = total.astype(BF16)
        send(reduce_copy(kind, h))

    make_partner(3)
    make_partner(-3)
    make_partner(4)
    make_own(3)
    make_own(-3)
    pair_copy(3).wait_recv()
    reduce_send(0, 0)
    pair_copy(-3).wait_recv()
    reduce_send(1, 0)
    make_own(4)
    pair_copy(4).wait_recv()
    reduce_send(3, 0)
    reduce_send(0, 1)
    reduce_send(2, 1)
    reduce_send(1, 1)
    make_partner(1)
    make_partner(-1)
    make_partner(2)
    make_partner(-2)
    make_own(1)
    make_own(-1)
    pair_copy(1).wait_recv()
    pair_copy(-1).wait_recv()
    for h in range(2):
        reduce_send(4, h)
        reduce_send(5, h)
    make_own(2)
    make_own(-2)
    make_partner(0)
    pair_copy(2).wait_recv()
    pair_copy(-2).wait_recv()

    def back_copy(h, i):
        to = (s + i) & (n_slab - 1)
        return remote(bsend.at[h, to], brecv.at[h, s], b_ss.at[h], b_rs.at[h], (to, a))

    weights_t = tilt_weights(
        lax.rem(iota((BOX, 2 * GPAD), 1), GPAD), iota((BOX, 2 * GPAD), 0), first_row(a) + s
    )

    def all_back(h):
        peers = pl.ds(0, n_slab - 1)
        return remote(bsend.at[h, peers], brecv.at[h, peers], b_ss.at[h], b_rs.at[h], partner)

    def own_copy(h):
        return pltpu.make_async_copy(bsend.at[h, s], brecv.at[h, s], img_sem.at[h])

    def round_two(h):
        reduce_send(6, h, (0, 2) if h == 1 else (0,))
        reduce_send(7, h, (1, 3) if h == 0 else (1,))

    def back_project(h):
        total = pair_sum(0, h)
        for kind in range(4, 8):
            reduce_copy(kind, h).wait_recv()
            total = total + rrecv[kind, h].astype(F32)
        total = unpack(total)
        high = total.astype(BF16)
        low = (total - high.astype(F32)).astype(BF16)
        back = dot_nn(weights_t, jnp.concatenate([high, low], axis=0)).astype(BF16)
        bsend[h] = back.reshape(n_slab, 16, BOX)
        for i in far_first:
            back_copy(h, i).start()
        own_copy(h).start()

    round_two(0)
    make_own(0)
    round_two(1)
    pair_copy(0).wait_recv()
    back_project(0)
    back_project(1)
    post_copy.wait()
    drain()
    for h in range(2):
        own_copy(h).wait()
        all_back(h).wait_send()
        all_back(h).wait_recv()


def on_device(n_slab, n_align, volume, images, orient, defocus, particle_counts):
    slots = images.shape[0]
    cols = 2 * BOX
    n_chunks = 8
    dma = pltpu.SemaphoreType.DMA
    hbm = pl.BlockSpec(memory_space=pltpu.HBM)
    planes, posterior = pl.pallas_call(
        functools.partial(kernel, n_slab, n_align),
        out_shape=(
            jax.ShapeDtypeStruct((2, n_slab, 16, BOX), BF16),
            jax.ShapeDtypeStruct((CAND, slots), F32),
        ),
        in_specs=[pl.BlockSpec(memory_space=pltpu.SMEM), hbm, hbm, hbm, hbm],
        out_specs=(hbm, hbm),
        scratch_shapes=[
            pltpu.VMEM((slots, ROWS, cols), BF16),
            pltpu.VMEM((ROWS, slots, cols + BOX), BF16),
            pltpu.VMEM((256, 256), BF16),
            pltpu.VMEM((16, ROWS, cols), BF16),
            pltpu.VMEM((CAND, slots), jnp.int32),
            pltpu.VMEM((slots,), BF16),
            pltpu.VMEM((slots, 128), F32),
            pltpu.VMEM((2, ROWS, 16, BOX), BF16),
            pltpu.VMEM((2, n_slab, 16, BOX), BF16),
            pltpu.VMEM((ROWS, 2, PIECE, 128), BF16),
            pltpu.VMEM((slots, 128), F32),
            pltpu.VMEM((slots, 128), F32),
            pltpu.VMEM((n_align, CAND, slots), F32),
            pltpu.VMEM((CHIPS, 2, PIECE, 128), F32),
            pltpu.VMEM((CHIPS, 2, PIECE, 128), BF16),
            pltpu.VMEM((CHIPS, 2, PIECE, 128), BF16),
            pltpu.VMEM((8, 2, PIECE, 128), BF16),
            pltpu.VMEM((8, 2, PIECE, 128), BF16),
            pltpu.VMEM((2, n_slab, 16, BOX), BF16),
            pltpu.VMEM((CAND, slots), F32),
            dma((n_chunks,)),
            dma((5,)),
            dma((2,)),
            dma((2,)),
            dma((8, 2)),
            dma((8, 2)),
            dma((CHIPS, 2)),
            dma((CHIPS, 2)),
            dma((1,)),
            dma((1,)),
            dma((CHIPS,)),
            dma((CHIPS,)),
            dma((8, 2)),
            dma((8, 2)),
            dma((2,)),
            dma((2,)),
        ],
        compiler_params=pltpu.CompilerParams(
            collective_id=0, has_side_effects=True, vmem_limit_bytes=60 * 1024 * 1024
        ),
    )(particle_counts, orient.T, defocus, volume, images)
    back_projection, posterior = pl.pallas_call(
        turn,
        out_shape=(
            jax.ShapeDtypeStruct((16, ROWS, cols), F32),
            jax.ShapeDtypeStruct((CAND, slots), F32),
        ),
        in_specs=[hbm, hbm],
        out_specs=(hbm, hbm),
        scratch_shapes=[
            pltpu.VMEM((2, n_slab, 16, BOX), BF16),
            pltpu.VMEM((16, ROWS, cols), F32),
            dma((5,)),
        ],
        compiler_params=pltpu.CompilerParams(vmem_limit_bytes=60 * 1024 * 1024),
    )(planes, posterior)
    return back_projection, posterior.T


def solution(mesh):
    return jax.shard_map(
        functools.partial(on_device, mesh.shape["slab"], mesh.shape["align"]),
        mesh=mesh,
        in_specs=(
            P("slab", "align", None),
            P("slab", "align", None),
            P("slab", None),
            P("slab"),
            P("slab"),
        ),
        out_specs=(P("slab", "align", None), P("slab", None)),
        check_vma=False,
    )
```

```python
import functools

import jax
import jax.numpy as jnp
from jax import lax
from jax.experimental import pallas as pl
from jax.experimental.pallas import tpu as pltpu
from jax.sharding import PartitionSpec as P

BOX = 256
TILT_STEPS = 32
GRID = 65
CAND = 8
GPAD = 80
BLOCK = 16
ROWS = 16
CHIPS = 8
PIECE = 144
MAIN = 128
CTF_PHASE = 0.1
MESH = pl.DeviceIdType.MESH
BF16 = jnp.bfloat16
F32 = jnp.float32

GATHER = ((2, 0), (-2, 0), (1, 0), (-1, 0), (1, -2), (-1, 2), (2, -2), (-2, 2))
REDUCE = ((1, 3), (-1, -3), (2, 4), (-2, 4), (1, 1), (-1, -1), (2, 2), (-2, -2))


def first_row(align):
    return align * ROWS


def sin_cos(angle):
    turns = jnp.floor(angle * F32(0.15915494309189535) + F32(0.5))
    half = ((angle - turns * F32(6.28125)) - turns * F32(0.0019353071795864769)) * F32(0.5)
    sq = half * half
    s = F32(-1.0 / 39916800.0)
    for coefficient in (1.0 / 362880.0, -1.0 / 5040.0, 1.0 / 120.0, -1.0 / 6.0, 1.0):
        s = s * sq + F32(coefficient)
    s = s * half
    c = F32(1.0 / 479001600.0)
    for coefficient in (-1.0 / 3628800.0, 1.0 / 40320.0, -1.0 / 720.0, 1.0 / 24.0, -0.5, 1.0):
        c = c * sq + F32(coefficient)
    return F32(2.0) * s * c, F32(1.0) - F32(2.0) * s * s


def tilt_weights(g, plane, ky):
    offset = (g - TILT_STEPS) * (ky - BOX // 2)
    lower = (BOX // 2 + lax.shift_right_arithmetic(offset, 5)) & (BOX - 1)
    upper = (lower + 1) & (BOX - 1)
    fraction = (offset & (TILT_STEPS - 1)).astype(F32) * F32(1.0 / TILT_STEPS)
    zero = jnp.zeros_like(fraction)
    weights = jnp.where(plane == lower, F32(1.0) - fraction, zero) + jnp.where(plane == upper, fraction, zero)
    return jnp.where(g < GRID, weights, zero).astype(BF16)


def iota(shape, axis):
    return lax.broadcasted_iota(jnp.int32, shape, axis)


def dot_nt(a, b):
    return lax.dot_general(a, b, (((1,), (1,)), ((), ())), preferred_element_type=F32)


def dot_nn(a, b):
    return jnp.dot(a, b, preferred_element_type=F32)


def pack(x):
    left, right = x[GRID - 1 :, :128], x[GRID - 1 :, 128:]
    row = iota(left.shape, 0)
    zero = jnp.zeros_like(left)
    last = jnp.where(row == 0, left, jnp.where(row == 1, pltpu.roll(right, 1, 0), zero))
    return jnp.concatenate([x[: GRID - 1, :128], x[: GRID - 1, 128:], last], axis=0)


def unpack(x):
    n = GRID - 1
    last = x[2 * n :]
    top = jnp.concatenate([x[:n], x[n : 2 * n]], axis=1)
    return jnp.concatenate(
        [top, jnp.concatenate([last, pltpu.roll(last, last.shape[0] - 1, 0)], axis=1)], axis=0
    )


def turn_back(last):
    return pltpu.roll(last, last.shape[0] - 2, 0)


def swap_matrix():
    r = iota((256, 256), 0)
    c = iota((256, 256), 1)
    swap = (lax.shift_right_logical(r, 4) == (c & 15)) & ((r & 15) == lax.shift_right_logical(c, 4))
    return jnp.where(swap, F32(1.0), F32(0.0)).astype(BF16)


def turn(planes_hbm, posterior_hbm, bp_hbm, post_hbm, planes_ref, bp_ref, sems):
    def copy_in(h):
        return pltpu.make_async_copy(planes_hbm.at[h], planes_ref.at[h], sems.at[h])

    def copy_out(h):
        part = pl.ds(h * BOX, BOX)
        return pltpu.make_async_copy(bp_ref.at[:, :, part], bp_hbm.at[:, :, part], sems.at[2 + h])

    post_copy = pltpu.make_async_copy(posterior_hbm, post_hbm, sems.at[4])
    copy_in(0).start()
    copy_in(1).start()
    post_copy.start()
    swap = swap_matrix()
    for h in range(2):
        copy_in(h).wait()
        turned = dot_nn(swap, planes_ref[h].reshape(256, BOX))
        bp_ref[:, :, h * BOX : (h + 1) * BOX] = turned.reshape(16, ROWS, BOX)
        copy_out(h).start()
    for h in range(2):
        copy_out(h).wait()
    post_copy.wait()


def kernel(
    n_slab, n_align, count_ref, orient_hbm, defocus_hbm, vol_hbm, img_ref, brecv, post_hbm,
    img_buf, lhs, perm, vol_ref, orient_ref, defocus_ref, dcol, volt, planes, sec, dist, energy, pick,
    osum, psend, precv, rsend, rrecv, bsend, post_ref,
    img_sem, in_sem, a2a_send, a2a_recv, g_ss, g_rs, pt_ss, pt_rs,
    ps_ss, ps_rs, rp_ss, rp_rs, r_ss, r_rs, b_ss, b_rs,
):
    s = lax.axis_index("slab")
    a = lax.axis_index("align")
    z = lax.shift_right_logical(s, 1)
    k = s & 1
    slots = lhs.shape[1]
    cols = 2 * BOX

    def slab_of(offset, core):
        return 2 * ((z + offset % CHIPS) & (CHIPS - 1)) + core

    partner = (2 * z + 1 - k, a)
    sent = []
    far_first = sorted(range(1, n_slab), key=lambda i: -min(i, n_slab - i))

    def remote(src, dst, send_sem, recv_sem, device):
        return pltpu.make_async_remote_copy(
            src_ref=src, dst_ref=dst, send_sem=send_sem, recv_sem=recv_sem, device_id=device, device_id_type=MESH
        )

    def send(copy):
        copy.start()
        sent.append(copy)

    def drain():
        for copy in sent:
            copy.wait_send()
        sent.clear()

    vol_copy = pltpu.make_async_copy(vol_hbm, vol_ref, in_sem.at[0])
    vol_copy.start()
    defocus_copy = pltpu.make_async_copy(defocus_hbm, defocus_ref, in_sem.at[2])
    defocus_copy.start()
    barrier = pltpu.get_barrier_semaphore()
    for i in far_first:
        pl.semaphore_signal(barrier, inc=1, device_id=((s + i) & (n_slab - 1), a), device_id_type=MESH)
    for i in range(1, n_align):
        pl.semaphore_signal(barrier, inc=1, device_id=(s, (a + i) & (n_align - 1)), device_id_type=MESH)

    n_chunks = img_sem.shape[0]
    chunk = slots // n_chunks

    def image_copy(i):
        part = pl.ds(i * chunk, chunk)
        return pltpu.make_async_copy(img_ref.at[part], img_buf.at[part], img_sem.at[i])


    def half(h):
        return slice(h * BOX, (h + 1) * BOX)

    perm[...] = swap_matrix()
    vol_copy.wait()
    for h in range(2):
        turned = dot_nn(perm[...], vol_ref[:, :, half(h)].reshape(256, BOX))
        volt[h] = turned.astype(BF16).reshape(ROWS, 16, BOX)

    pl.semaphore_wait(barrier, n_slab + n_align - 2)

    def plane_copy(h, i):
        to = (s + i) & (n_slab - 1)
        return remote(volt.at[h, to], planes.at[h, s], a2a_send.at[h], a2a_recv.at[h], (to, a))

    def all_planes(h):
        peers = pl.ds(0, n_slab - 1)
        return remote(volt.at[h, peers], planes.at[h, peers], a2a_send.at[h], a2a_recv.at[h], partner)

    for h in range(2):
        for i in far_first:
            plane_copy(h, i).start()
    for i in range(n_chunks):
        image_copy(i).start()
    orient_copy = pltpu.make_async_copy(orient_hbm, orient_ref, in_sem.at[1])
    orient_copy.start()
    for h in range(2):
        planes[h, s] = volt[h, s]

    defocus_copy.wait()
    dcol[...] = lax.dot_general(
        defocus_ref[...].reshape(1, slots), jnp.ones((1, 128), BF16), (((0,), (0,)), ((), ())), preferred_element_type=F32
    )
    kx = (iota((BLOCK, BOX), 1) - BOX // 2).astype(F32)
    kx2 = kx * kx * F32(1.0 / (BOX * BOX))
    ky = ((iota((BLOCK, 128), 1) & (ROWS - 1)) + first_row(a) - BOX // 2).astype(F32)
    ky2 = ky * ky * F32(1.0 / (BOX * BOX))

    def ctf_block(first):
        at = pl.ds(pl.multiple_of(first, BLOCK), BLOCK)
        defocus = dcol[at, :]
        sin_x, cos_x = sin_cos(jnp.concatenate([defocus, defocus], axis=1) * kx2)
        sin_y, cos_y = sin_cos(defocus * ky2 + F32(CTF_PHASE))
        rows = dot_nn(perm[...], img_buf[at].reshape(256, cols))
        total = jnp.zeros((BLOCK, BOX), F32)
        for row in range(ROWS):
            wave = sin_x * cos_y[:, row : row + 1] + cos_x * sin_y[:, row : row + 1]
            real = rows[row * BLOCK : (row + 1) * BLOCK, :BOX]
            imag = rows[row * BLOCK : (row + 1) * BLOCK, BOX:]
            total = total + (real * real + imag * imag)
            lhs[row, at, 0:BOX] = (wave * real).astype(BF16)
            lhs[row, at, BOX:cols] = (wave * imag).astype(BF16)
            lhs[row, at, cols : cols + BOX] = (wave * wave).astype(BF16)
        energy[at, :] = total[:, :128] + total[:, 128:]

    def ctf_chunks(low, high):
        @pl.loop(low, high)
        def _(i):
            image_copy(i).wait()

            @pl.loop(0, chunk // (2 * BLOCK))
            def _(j):
                for u in range(2):
                    ctf_block(i * chunk + (2 * j + u) * BLOCK)

    def gather_copy(kind, h):
        to, owner = GATHER[kind]
        row = slab_of(owner, k)
        part = sec.at[row, h, pl.ds(0, PIECE if h == 1 else MAIN)]
        return remote(part, part, g_ss.at[kind, h], g_rs.at[kind, h], (slab_of(to, k), a))

    def relay_copy(offset, h):
        row = slab_of(offset, k)
        slot = offset % CHIPS
        part = sec.at[row, h, pl.ds(0, PIECE if h == 1 else MAIN)]
        return remote(part, part, pt_ss.at[slot, h], pt_rs.at[slot, h], partner)

    cuts = (0, 5 * n_chunks // 8, n_chunks, n_chunks)
    weights = tilt_weights(iota((GPAD, BOX), 0), iota((GPAD, BOX), 1), first_row(a) + s)
    for h in range(2):
        ctf_chunks(cuts[h], cuts[h + 1])
        all_planes(h).wait_recv()
        packed = pack(dot_nn(weights, planes[h].reshape(BOX, BOX)))
        sec[s, h, :MAIN] = packed[:MAIN].astype(BF16)
        if h == 0:
            last = packed[MAIN:]
        else:
            sec[s, h, MAIN:] = (packed[MAIN:] + pltpu.roll(last, 2, 0)).astype(BF16)
        for kind in range(4):
            send(gather_copy(kind, h))
        send(relay_copy(0, h))

    def operand(row):
        both = sec[row, 1].astype(F32)
        real = unpack(jnp.concatenate([sec[row, 0, :MAIN].astype(F32), turn_back(both[MAIN:])], axis=0))
        imag = unpack(both)
        square = (real * real + imag * imag).astype(BF16)
        return jnp.concatenate(
            [(real * F32(-2.0)).astype(BF16), (imag * F32(-2.0)).astype(BF16), square], axis=1
        )

    def score(row):
        return dot_nt(lhs[row], operand(row))

    def row_at(offset, core):
        return 2 * ((z + CHIPS + offset) & (CHIPS - 1)) + core

    def forward(h):
        gather_copy(0, h).wait_recv()
        send(gather_copy(4, h))
        if h == 0:
            send(gather_copy(6, h))
        send(relay_copy(-2, h))
        gather_copy(1, h).wait_recv()
        send(gather_copy(5, h))
        if h == 1:
            send(gather_copy(7, h))
        send(relay_copy(2, h))

    def add_scores(offsets, core):
        if len(offsets) == 1:
            dist[:, :GPAD] += score(row_at(offsets[0], core))
        else:
            @pl.loop(0, len(offsets) // 2)
            def _(i):
                near = offsets[-1] - i
                dist[:, :GPAD] += score(row_at(near, core)) + score(row_at(-near, core))

    for i in range(CHIPS):
        psend[i, 1, MAIN:] = jnp.zeros((PIECE - MAIN, 128), BF16)
    forward(0)
    dist[...] = jnp.zeros_like(dist) + jnp.sum(energy[...], axis=1, keepdims=True)
    add_scores([0], k)
    forward(1)
    for h in range(2):
        gather_copy(2, h).wait_recv()
        send(relay_copy(-1, h))
        gather_copy(3, h).wait_recv()
        send(relay_copy(1, h))
    add_scores([-2, -1, 1, 2], k)
    for offset in (0, -2, 2, -1, 1):
        for h in range(2):
            relay_copy(offset, h).wait_recv()
    add_scores([0], 1 - k)
    for h in range(2):
        gather_copy(4, h).wait_recv()
        send(relay_copy(-3, h))
        gather_copy(5, h).wait_recv()
        send(relay_copy(3, h))
        gather_copy(6 + h, h).wait_recv()
        send(relay_copy(4, h))
    add_scores([-2, -1, 1, 2], 1 - k)
    add_scores([-3, 3], k)
    add_scores([4], k)
    for offset in (-3, 3, 4):
        for h in range(2):
            relay_copy(offset, h).wait_recv()
    add_scores([-3, 3], 1 - k)
    add_scores([4], 1 - k)

    orient_copy.wait()
    orient = orient_ref[...]
    full_t = dist[...].T[:GPAD]
    g_ids = iota((GPAD, slots), 0)
    for n in range(CAND):
        chosen = orient[n : n + 1, :] == g_ids
        pick[a, n : n + 1, :] = jnp.sum(jnp.where(chosen, full_t, F32(0.0)), axis=0, keepdims=True)

    def pick_copy(i):
        to = (a + i) & (n_align - 1)
        return remote(pick.at[a], pick.at[a], ps_ss.at[0], ps_rs.at[0], (s, to))

    def all_picks():
        peers = pl.ds(0, n_align - 1)
        return remote(pick.at[peers], pick.at[peers], ps_ss.at[0], ps_rs.at[0], partner)

    for i in range(1, n_align):
        pick_copy(i).start()
    for h in range(2):
        all_planes(h).wait_send()
    drain()
    if n_align > 1:
        all_picks().wait_recv()
        all_picks().wait_send()
    picked = pick[0]
    for i in range(1, n_align):
        picked = picked + pick[i]
    scores = picked * F32(-1.0 / BOX)
    e = jnp.exp(scores - jnp.max(scores, axis=0, keepdims=True))
    posterior = e / jnp.sum(e, axis=0, keepdims=True)
    posterior = jnp.where(iota((CAND, slots), 1) < count_ref[0], posterior, F32(0.0))
    post_ref[...] = posterior
    post_copy = pltpu.make_async_copy(post_ref, post_hbm, in_sem.at[3])
    post_copy.start()
    per_grid = jnp.zeros((GPAD, slots), F32)
    for n in range(CAND):
        chosen = orient[n : n + 1, :] == g_ids
        per_grid = per_grid + jnp.where(chosen, posterior[n : n + 1, :], F32(0.0))
    per_grid = per_grid.astype(BF16)

    def pair_copy(offset):
        i = offset % CHIPS
        return remote(psend.at[i], precv.at[i], rp_ss.at[i], rp_rs.at[i], partner)

    def size(h):
        return PIECE if h == 0 else MAIN

    def pack_both(total):
        real, imag = pack(total[:, :BOX]), pack(total[:, BOX:])
        last = real[MAIN:] + pltpu.roll(imag[MAIN:], 2, 0)
        return jnp.concatenate([real[:MAIN], last], axis=0), imag[:MAIN]

    def make_partner(offset):
        total = dot_nn(per_grid, lhs[slab_of(offset, 1 - k), :, 0:cols])
        for h, packed in enumerate(pack_both(total)):
            psend[offset % CHIPS, h, : size(h)] = packed.astype(BF16)
        send(pair_copy(offset))

    def make_own(offset):
        total = dot_nn(per_grid, lhs[slab_of(offset, k), :, 0:cols])
        for h, packed in enumerate(pack_both(total)):
            osum[offset % CHIPS, h, : size(h)] = packed

    def pair_sum(offset, h):
        i, part = offset % CHIPS, slice(0, size(h))
        return osum[i, h, part] + precv[i, h, part].astype(F32)

    def reduce_copy(kind, h):
        to = (slab_of(REDUCE[kind][0], k), a)
        part = pl.ds(0, size(h))
        return remote(
            rsend.at[kind, h, part], rrecv.at[kind, h, part], r_ss.at[kind, h], r_rs.at[kind, h], to
        )

    def reduce_send(kind, h, extra=()):
        total = pair_sum(REDUCE[kind][1], h)
        for other in extra:
            reduce_copy(other, h).wait_recv()
            total = total + rrecv[other, h, : size(h)].astype(F32)
        rsend[kind, h, : size(h)] = total.astype(BF16)
        send(reduce_copy(kind, h))

    make_partner(3)
    make_partner(-3)
    make_partner(4)
    make_own(3)
    make_own(-3)
    pair_copy(3).wait_recv()
    reduce_send(0, 0)
    pair_copy(-3).wait_recv()
    reduce_send(1, 0)
    make_own(4)
    pair_copy(4).wait_recv()
    reduce_send(3, 0)
    reduce_send(0, 1)
    reduce_send(2, 1)
    reduce_send(1, 1)
    make_partner(1)
    make_partner(-1)
    make_partner(2)
    make_partner(-2)
    make_own(1)
    make_own(-1)
    pair_copy(1).wait_recv()
    pair_copy(-1).wait_recv()
    for h in range(2):
        reduce_send(4, h)
        reduce_send(5, h)
    make_own(2)
    make_own(-2)
    make_partner(0)
    pair_copy(2).wait_recv()
    pair_copy(-2).wait_recv()

    def back_copy(h, i):
        to = (s + i) & (n_slab - 1)
        return remote(bsend.at[h, to], brecv.at[h, s], b_ss.at[h], b_rs.at[h], (to, a))

    weights_t = tilt_weights(
        lax.rem(iota((BOX, 2 * GPAD), 1), GPAD), iota((BOX, 2 * GPAD), 0), first_row(a) + s
    )

    def all_back(h):
        peers = pl.ds(0, n_slab - 1)
        return remote(bsend.at[h, peers], brecv.at[h, peers], b_ss.at[h], b_rs.at[h], partner)

    def own_copy(h):
        return pltpu.make_async_copy(bsend.at[h, s], brecv.at[h, s], img_sem.at[h])

    def round_two(h):
        reduce_send(6, h, (0, 2) if h == 1 else (0,))
        reduce_send(7, h, (1, 3) if h == 0 else (1,))

    def back_project(h, last=None):
        total = pair_sum(0, h)
        for kind in range(4, 8):
            reduce_copy(kind, h).wait_recv()
            total = total + rrecv[kind, h, : size(h)].astype(F32)
        if h == 0:
            last = turn_back(total[MAIN:])
        else:
            total = jnp.concatenate([total, last], axis=0)
        total = unpack(total)
        high = total.astype(BF16)
        low = (total - high.astype(F32)).astype(BF16)
        back = dot_nn(weights_t, jnp.concatenate([high, low], axis=0)).astype(BF16)
        bsend[h] = back.reshape(n_slab, 16, BOX)
        for i in far_first:
            back_copy(h, i).start()
        own_copy(h).start()
        return last

    round_two(0)
    make_own(0)
    round_two(1)
    pair_copy(0).wait_recv()
    back_project(1, back_project(0))
    post_copy.wait()
    drain()
    for h in range(2):
        own_copy(h).wait()
        all_back(h).wait_send()
        all_back(h).wait_recv()


def on_device(n_slab, n_align, volume, images, orient, defocus, particle_counts):
    slots = images.shape[0]
    cols = 2 * BOX
    n_chunks = 8
    dma = pltpu.SemaphoreType.DMA
    hbm = pl.BlockSpec(memory_space=pltpu.HBM)
    planes, posterior = pl.pallas_call(
        functools.partial(kernel, n_slab, n_align),
        out_shape=(
            jax.ShapeDtypeStruct((2, n_slab, 16, BOX), BF16),
            jax.ShapeDtypeStruct((CAND, slots), F32),
        ),
        in_specs=[pl.BlockSpec(memory_space=pltpu.SMEM), hbm, hbm, hbm, hbm],
        out_specs=(hbm, hbm),
        scratch_shapes=[
            pltpu.VMEM((slots, ROWS, cols), BF16),
            pltpu.VMEM((ROWS, slots, cols + BOX), BF16),
            pltpu.VMEM((256, 256), BF16),
            pltpu.VMEM((16, ROWS, cols), BF16),
            pltpu.VMEM((CAND, slots), jnp.int32),
            pltpu.VMEM((slots,), BF16),
            pltpu.VMEM((slots, 128), F32),
            pltpu.VMEM((2, ROWS, 16, BOX), BF16),
            pltpu.VMEM((2, n_slab, 16, BOX), BF16),
            pltpu.VMEM((ROWS, 2, PIECE, 128), BF16),
            pltpu.VMEM((slots, 128), F32),
            pltpu.VMEM((slots, 128), F32),
            pltpu.VMEM((n_align, CAND, slots), F32),
            pltpu.VMEM((CHIPS, 2, PIECE, 128), F32),
            pltpu.VMEM((CHIPS, 2, PIECE, 128), BF16),
            pltpu.VMEM((CHIPS, 2, PIECE, 128), BF16),
            pltpu.VMEM((8, 2, PIECE, 128), BF16),
            pltpu.VMEM((8, 2, PIECE, 128), BF16),
            pltpu.VMEM((2, n_slab, 16, BOX), BF16),
            pltpu.VMEM((CAND, slots), F32),
            dma((n_chunks,)),
            dma((5,)),
            dma((2,)),
            dma((2,)),
            dma((8, 2)),
            dma((8, 2)),
            dma((CHIPS, 2)),
            dma((CHIPS, 2)),
            dma((1,)),
            dma((1,)),
            dma((CHIPS,)),
            dma((CHIPS,)),
            dma((8, 2)),
            dma((8, 2)),
            dma((2,)),
            dma((2,)),
        ],
        compiler_params=pltpu.CompilerParams(
            collective_id=0, has_side_effects=True, vmem_limit_bytes=60 * 1024 * 1024
        ),
    )(particle_counts, orient.T, defocus, volume, images)
    back_projection, posterior = pl.pallas_call(
        turn,
        out_shape=(
            jax.ShapeDtypeStruct((16, ROWS, cols), F32),
            jax.ShapeDtypeStruct((CAND, slots), F32),
        ),
        in_specs=[hbm, hbm],
        out_specs=(hbm, hbm),
        scratch_shapes=[
            pltpu.VMEM((2, n_slab, 16, BOX), BF16),
            pltpu.VMEM((16, ROWS, cols), F32),
            dma((5,)),
        ],
        compiler_params=pltpu.CompilerParams(vmem_limit_bytes=60 * 1024 * 1024),
    )(planes, posterior)
    return back_projection, posterior.T


def solution(mesh):
    return jax.shard_map(
        functools.partial(on_device, mesh.shape["slab"], mesh.shape["align"]),
        mesh=mesh,
        in_specs=(
            P("slab", "align", None),
            P("slab", "align", None),
            P("slab", None),
            P("slab"),
            P("slab"),
        ),
        out_specs=(P("slab", "align", None), P("slab", None)),
        check_vma=False,
    )
```

```python
import functools

import jax
import jax.numpy as jnp
from jax import lax
from jax.experimental import pallas as pl
from jax.experimental.pallas import tpu as pltpu
from jax.sharding import PartitionSpec as P

BOX = 256
TILT_STEPS = 32
GRID = 65
CAND = 8
GPAD = 80
BLOCK = 16
ROWS = 16
CHIPS = 8
PIECE = 144
MAIN = 128
CTF_PHASE = 0.1
MESH = pl.DeviceIdType.MESH
BF16 = jnp.bfloat16
F32 = jnp.float32

GATHER = ((2, 0), (-2, 0), (1, 0), (-1, 0), (1, -2), (-1, 2), (2, -2), (-2, 2))
REDUCE = ((1, 3), (-1, -3), (2, 4), (-2, 4), (1, 1), (-1, -1), (2, 2), (-2, -2))


def first_row(align):
    return align * ROWS


def sin_cos(angle):
    turns = jnp.floor(angle * F32(0.15915494309189535) + F32(0.5))
    half = ((angle - turns * F32(6.28125)) - turns * F32(0.0019353071795864769)) * F32(0.5)
    sq = half * half
    s = F32(-1.0 / 39916800.0)
    for coefficient in (1.0 / 362880.0, -1.0 / 5040.0, 1.0 / 120.0, -1.0 / 6.0, 1.0):
        s = s * sq + F32(coefficient)
    s = s * half
    c = F32(1.0 / 479001600.0)
    for coefficient in (-1.0 / 3628800.0, 1.0 / 40320.0, -1.0 / 720.0, 1.0 / 24.0, -0.5, 1.0):
        c = c * sq + F32(coefficient)
    return F32(2.0) * s * c, F32(1.0) - F32(2.0) * s * s


def tilt_weights(g, plane, ky):
    offset = (g - TILT_STEPS) * (ky - BOX // 2)
    lower = (BOX // 2 + lax.shift_right_arithmetic(offset, 5)) & (BOX - 1)
    upper = (lower + 1) & (BOX - 1)
    fraction = (offset & (TILT_STEPS - 1)).astype(F32) * F32(1.0 / TILT_STEPS)
    zero = jnp.zeros_like(fraction)
    weights = jnp.where(plane == lower, F32(1.0) - fraction, zero) + jnp.where(plane == upper, fraction, zero)
    return jnp.where(g < GRID, weights, zero).astype(BF16)


def iota(shape, axis):
    return lax.broadcasted_iota(jnp.int32, shape, axis)


def dot_nt(a, b):
    return lax.dot_general(a, b, (((1,), (1,)), ((), ())), preferred_element_type=F32)


def dot_nn(a, b):
    return jnp.dot(a, b, preferred_element_type=F32)


def pack(x):
    left, right = x[GRID - 1 :, :128], x[GRID - 1 :, 128:]
    row = iota(left.shape, 0)
    zero = jnp.zeros_like(left)
    last = jnp.where(row == 0, left, jnp.where(row == 1, pltpu.roll(right, 1, 0), zero))
    return jnp.concatenate([x[: GRID - 1, :128], x[: GRID - 1, 128:], last], axis=0)


def unpack(x):
    n = GRID - 1
    last = x[2 * n :]
    top = jnp.concatenate([x[:n], x[n : 2 * n]], axis=1)
    return jnp.concatenate(
        [top, jnp.concatenate([last, pltpu.roll(last, last.shape[0] - 1, 0)], axis=1)], axis=0
    )


def turn_back(last):
    return pltpu.roll(last, last.shape[0] - 2, 0)


def swap_matrix():
    r = iota((256, 256), 0)
    c = iota((256, 256), 1)
    swap = (lax.shift_right_logical(r, 4) == (c & 15)) & ((r & 15) == lax.shift_right_logical(c, 4))
    return jnp.where(swap, F32(1.0), F32(0.0)).astype(BF16)


def turn(planes_hbm, posterior_hbm, bp_hbm, post_hbm, planes_ref, bp_ref, sems):
    def copy_in(h):
        return pltpu.make_async_copy(planes_hbm.at[h], planes_ref.at[h], sems.at[h])

    def copy_out(h):
        part = pl.ds(h * BOX, BOX)
        return pltpu.make_async_copy(bp_ref.at[:, :, part], bp_hbm.at[:, :, part], sems.at[2 + h])

    post_copy = pltpu.make_async_copy(posterior_hbm, post_hbm, sems.at[4])
    copy_in(0).start()
    copy_in(1).start()
    post_copy.start()
    swap = swap_matrix()
    for h in range(2):
        copy_in(h).wait()
        turned = dot_nn(swap, planes_ref[h].reshape(256, BOX))
        bp_ref[:, :, h * BOX : (h + 1) * BOX] = turned.reshape(16, ROWS, BOX)
        copy_out(h).start()
    for h in range(2):
        copy_out(h).wait()
    post_copy.wait()


def kernel(
    n_slab, n_align, count_ref, orient_hbm, defocus_hbm, vol_hbm, img_ref, brecv, post_hbm,
    img_buf, lhs, perm, vol_ref, orient_ref, defocus_ref, dcol, volt, planes, sec, dist, energy, pick,
    osum, psend, precv, rsend, rrecv, bsend, post_ref,
    img_sem, in_sem, a2a_send, a2a_recv, g_ss, g_rs, pt_ss, pt_rs,
    ps_ss, ps_rs, rp_ss, rp_rs, r_ss, r_rs, b_ss, b_rs,
):
    s = lax.axis_index("slab")
    a = lax.axis_index("align")
    z = lax.shift_right_logical(s, 1)
    k = s & 1
    slots = lhs.shape[1]
    cols = 2 * BOX

    def slab_of(offset, core):
        return 2 * ((z + offset % CHIPS) & (CHIPS - 1)) + core

    partner = (2 * z + 1 - k, a)
    sent = []
    far_first = sorted(range(1, n_slab), key=lambda i: -min(i, n_slab - i))

    def remote(src, dst, send_sem, recv_sem, device):
        return pltpu.make_async_remote_copy(
            src_ref=src, dst_ref=dst, send_sem=send_sem, recv_sem=recv_sem, device_id=device, device_id_type=MESH
        )

    def send(copy):
        copy.start()
        sent.append(copy)

    def drain():
        for copy in sent:
            copy.wait_send()
        sent.clear()

    vol_copy = pltpu.make_async_copy(vol_hbm, vol_ref, in_sem.at[0])
    vol_copy.start()
    defocus_copy = pltpu.make_async_copy(defocus_hbm, defocus_ref, in_sem.at[2])
    defocus_copy.start()
    barrier = pltpu.get_barrier_semaphore()
    for i in far_first:
        pl.semaphore_signal(barrier, inc=1, device_id=((s + i) & (n_slab - 1), a), device_id_type=MESH)
    for i in range(1, n_align):
        pl.semaphore_signal(barrier, inc=1, device_id=(s, (a + i) & (n_align - 1)), device_id_type=MESH)

    n_chunks = img_sem.shape[0]
    chunk = slots // n_chunks

    def image_copy(i):
        part = pl.ds(i * chunk, chunk)
        return pltpu.make_async_copy(img_ref.at[part], img_buf.at[part], img_sem.at[i])


    def half(h):
        return slice(h * BOX, (h + 1) * BOX)

    perm[...] = swap_matrix()
    vol_copy.wait()
    for h in range(2):
        turned = dot_nn(perm[...], vol_ref[:, :, half(h)].reshape(256, BOX))
        volt[h] = turned.astype(BF16).reshape(ROWS, 16, BOX)

    pl.semaphore_wait(barrier, n_slab + n_align - 2)

    def plane_copy(h, i):
        to = (s + i) & (n_slab - 1)
        return remote(volt.at[h, to], planes.at[h, s], a2a_send.at[h], a2a_recv.at[h], (to, a))

    def all_planes(h):
        peers = pl.ds(0, n_slab - 1)
        return remote(volt.at[h, peers], planes.at[h, peers], a2a_send.at[h], a2a_recv.at[h], partner)

    for h in range(2):
        for i in far_first:
            plane_copy(h, i).start()
    for i in range(n_chunks):
        image_copy(i).start()
    orient_copy = pltpu.make_async_copy(orient_hbm, orient_ref, in_sem.at[1])
    orient_copy.start()
    for h in range(2):
        planes[h, s] = volt[h, s]

    defocus_copy.wait()
    dcol[...] = lax.dot_general(
        defocus_ref[...].reshape(1, slots), jnp.ones((1, 128), BF16), (((0,), (0,)), ((), ())), preferred_element_type=F32
    )
    kx = (iota((BLOCK, BOX), 1) - BOX // 2).astype(F32)
    kx2 = kx * kx * F32(1.0 / (BOX * BOX))
    ky = ((iota((BLOCK, 128), 1) & (ROWS - 1)) + first_row(a) - BOX // 2).astype(F32)
    ky2 = ky * ky * F32(1.0 / (BOX * BOX))

    def ctf_block(first):
        at = pl.ds(pl.multiple_of(first, BLOCK), BLOCK)
        defocus = dcol[at, :]
        sin_x, cos_x = sin_cos(jnp.concatenate([defocus, defocus], axis=1) * kx2)
        sin_y, cos_y = sin_cos(defocus * ky2 + F32(CTF_PHASE))
        rows = dot_nn(perm[...], img_buf[at].reshape(256, cols))
        total = jnp.zeros((BLOCK, BOX), F32)
        for row in range(ROWS):
            wave = sin_x * cos_y[:, row : row + 1] + cos_x * sin_y[:, row : row + 1]
            real = rows[row * BLOCK : (row + 1) * BLOCK, :BOX]
            imag = rows[row * BLOCK : (row + 1) * BLOCK, BOX:]
            total = total + (real * real + imag * imag)
            lhs[row, at, 0:BOX] = (wave * real).astype(BF16)
            lhs[row, at, BOX:cols] = (wave * imag).astype(BF16)
            lhs[row, at, cols : cols + BOX] = (wave * wave).astype(BF16)
        energy[at, :] = total[:, :128] + total[:, 128:]

    def ctf_chunks(low, high):
        @pl.loop(low, high)
        def _(i):
            image_copy(i).wait()

            @pl.loop(0, chunk // (2 * BLOCK))
            def _(j):
                for u in range(2):
                    ctf_block(i * chunk + (2 * j + u) * BLOCK)

    def gather_copy(kind, h):
        to, owner = GATHER[kind]
        row = slab_of(owner, k)
        part = sec.at[row, h, pl.ds(0, PIECE if h == 1 else MAIN)]
        return remote(part, part, g_ss.at[kind, h], g_rs.at[kind, h], (slab_of(to, k), a))

    def relay_copy(offset, h):
        row = slab_of(offset, k)
        slot = offset % CHIPS
        part = sec.at[row, h, pl.ds(0, PIECE if h == 1 else MAIN)]
        return remote(part, part, pt_ss.at[slot, h], pt_rs.at[slot, h], partner)

    cuts = (0, 5 * n_chunks // 8, n_chunks, n_chunks)
    weights = tilt_weights(iota((GPAD, BOX), 0), iota((GPAD, BOX), 1), first_row(a) + s)
    for h in range(2):
        ctf_chunks(cuts[h], cuts[h + 1])
        all_planes(h).wait_recv()
        packed = pack(dot_nn(weights, planes[h].reshape(BOX, BOX)))
        sec[s, h, :MAIN] = packed[:MAIN].astype(BF16)
        if h == 0:
            last = packed[MAIN:]
        else:
            sec[s, h, MAIN:] = (packed[MAIN:] + pltpu.roll(last, 2, 0)).astype(BF16)
        for kind in range(4):
            send(gather_copy(kind, h))
        send(relay_copy(0, h))

    def operand(row):
        both = sec[row, 1].astype(F32)
        real = unpack(jnp.concatenate([sec[row, 0, :MAIN].astype(F32), turn_back(both[MAIN:])], axis=0))
        imag = unpack(both)
        square = (real * real + imag * imag).astype(BF16)
        return jnp.concatenate(
            [(real * F32(-2.0)).astype(BF16), (imag * F32(-2.0)).astype(BF16), square], axis=1
        )

    def score(row):
        return dot_nt(lhs[row], operand(row))

    def row_at(offset, core):
        return 2 * ((z + CHIPS + offset) & (CHIPS - 1)) + core

    def forward(h):
        gather_copy(0, h).wait_recv()
        if h == 0:
            send(gather_copy(6, h))
        send(gather_copy(4, h))
        send(relay_copy(-2, h))
        gather_copy(1, h).wait_recv()
        if h == 1:
            send(gather_copy(7, h))
        send(gather_copy(5, h))
        send(relay_copy(2, h))

    def add_scores(offsets, core):
        if len(offsets) == 1:
            dist[:, :GPAD] += score(row_at(offsets[0], core))
        else:
            @pl.loop(0, len(offsets) // 2)
            def _(i):
                near = offsets[-1] - i
                dist[:, :GPAD] += score(row_at(near, core)) + score(row_at(-near, core))

    for i in range(CHIPS):
        psend[i, 1, MAIN:] = jnp.zeros((PIECE - MAIN, 128), BF16)
    forward(0)
    dist[...] = jnp.zeros_like(dist) + jnp.sum(energy[...], axis=1, keepdims=True)
    add_scores([0], k)
    forward(1)
    for h in range(2):
        gather_copy(2, h).wait_recv()
        send(relay_copy(-1, h))
        gather_copy(3, h).wait_recv()
        send(relay_copy(1, h))
    add_scores([-2, -1, 1, 2], k)
    for offset in (0, -2, 2, -1, 1):
        for h in range(2):
            relay_copy(offset, h).wait_recv()
    add_scores([0], 1 - k)
    for h in range(2):
        gather_copy(4, h).wait_recv()
        send(relay_copy(-3, h))
        gather_copy(5, h).wait_recv()
        send(relay_copy(3, h))
        gather_copy(6 + h, h).wait_recv()
        send(relay_copy(4, h))
    add_scores([-2, -1, 1, 2], 1 - k)
    add_scores([-3, 3], k)
    add_scores([4], k)
    for offset in (-3, 3, 4):
        for h in range(2):
            relay_copy(offset, h).wait_recv()
    add_scores([-3, 3], 1 - k)
    add_scores([4], 1 - k)

    orient_copy.wait()
    orient = orient_ref[...]
    full_t = dist[...].T[:GPAD]
    g_ids = iota((GPAD, slots), 0)
    for n in range(CAND):
        chosen = orient[n : n + 1, :] == g_ids
        pick[a, n : n + 1, :] = jnp.sum(jnp.where(chosen, full_t, F32(0.0)), axis=0, keepdims=True)

    def pick_copy(i):
        to = (a + i) & (n_align - 1)
        return remote(pick.at[a], pick.at[a], ps_ss.at[0], ps_rs.at[0], (s, to))

    def all_picks():
        peers = pl.ds(0, n_align - 1)
        return remote(pick.at[peers], pick.at[peers], ps_ss.at[0], ps_rs.at[0], partner)

    for i in range(1, n_align):
        pick_copy(i).start()
    for h in range(2):
        all_planes(h).wait_send()
    drain()
    if n_align > 1:
        all_picks().wait_recv()
        all_picks().wait_send()
    picked = pick[0]
    for i in range(1, n_align):
        picked = picked + pick[i]
    scores = picked * F32(-1.0 / BOX)
    e = jnp.exp(scores - jnp.max(scores, axis=0, keepdims=True))
    posterior = e / jnp.sum(e, axis=0, keepdims=True)
    posterior = jnp.where(iota((CAND, slots), 1) < count_ref[0], posterior, F32(0.0))
    post_ref[...] = posterior
    post_copy = pltpu.make_async_copy(post_ref, post_hbm, in_sem.at[3])
    post_copy.start()
    per_grid = jnp.zeros((GPAD, slots), F32)
    for n in range(CAND):
        chosen = orient[n : n + 1, :] == g_ids
        per_grid = per_grid + jnp.where(chosen, posterior[n : n + 1, :], F32(0.0))
    per_grid = per_grid.astype(BF16)

    def pair_copy(offset):
        i = offset % CHIPS
        return remote(psend.at[i], precv.at[i], rp_ss.at[i], rp_rs.at[i], partner)

    def size(h):
        return PIECE if h == 0 else MAIN

    def pack_both(total):
        real, imag = pack(total[:, :BOX]), pack(total[:, BOX:])
        last = real[MAIN:] + pltpu.roll(imag[MAIN:], 2, 0)
        return jnp.concatenate([real[:MAIN], last], axis=0), imag[:MAIN]

    def make_partner(offset):
        total = dot_nn(per_grid, lhs[slab_of(offset, 1 - k), :, 0:cols])
        for h, packed in enumerate(pack_both(total)):
            psend[offset % CHIPS, h, : size(h)] = packed.astype(BF16)
        send(pair_copy(offset))

    def make_own(offset):
        total = dot_nn(per_grid, lhs[slab_of(offset, k), :, 0:cols])
        for h, packed in enumerate(pack_both(total)):
            osum[offset % CHIPS, h, : size(h)] = packed

    def pair_sum(offset, h):
        i, part = offset % CHIPS, slice(0, size(h))
        return osum[i, h, part] + precv[i, h, part].astype(F32)

    def reduce_copy(kind, h):
        to = (slab_of(REDUCE[kind][0], k), a)
        part = pl.ds(0, size(h))
        return remote(
            rsend.at[kind, h, part], rrecv.at[kind, h, part], r_ss.at[kind, h], r_rs.at[kind, h], to
        )

    def reduce_send(kind, h, extra=()):
        total = pair_sum(REDUCE[kind][1], h)
        for other in extra:
            reduce_copy(other, h).wait_recv()
            total = total + rrecv[other, h, : size(h)].astype(F32)
        rsend[kind, h, : size(h)] = total.astype(BF16)
        send(reduce_copy(kind, h))

    make_partner(3)
    make_partner(-3)
    make_partner(4)
    make_own(3)
    make_own(-3)
    pair_copy(3).wait_recv()
    reduce_send(0, 0)
    pair_copy(-3).wait_recv()
    reduce_send(1, 0)
    make_own(4)
    pair_copy(4).wait_recv()
    reduce_send(3, 0)
    reduce_send(0, 1)
    reduce_send(2, 1)
    reduce_send(1, 1)
    make_partner(1)
    make_partner(-1)
    make_partner(2)
    make_partner(-2)
    make_own(1)
    make_own(-1)
    pair_copy(1).wait_recv()
    pair_copy(-1).wait_recv()
    for h in range(2):
        reduce_send(4, h)
        reduce_send(5, h)
    make_own(2)
    make_own(-2)
    make_partner(0)
    pair_copy(2).wait_recv()
    pair_copy(-2).wait_recv()

    def back_copy(h, i):
        to = (s + i) & (n_slab - 1)
        return remote(bsend.at[h, to], brecv.at[h, s], b_ss.at[h], b_rs.at[h], (to, a))

    weights_t = tilt_weights(
        lax.rem(iota((BOX, 2 * GPAD), 1), GPAD), iota((BOX, 2 * GPAD), 0), first_row(a) + s
    )

    def all_back(h):
        peers = pl.ds(0, n_slab - 1)
        return remote(bsend.at[h, peers], brecv.at[h, peers], b_ss.at[h], b_rs.at[h], partner)

    def own_copy(h):
        return pltpu.make_async_copy(bsend.at[h, s], brecv.at[h, s], img_sem.at[h])

    def round_two(h):
        reduce_send(6, h, (0, 2) if h == 1 else (0,))
        reduce_send(7, h, (1, 3) if h == 0 else (1,))

    def back_project(h, last=None):
        total = pair_sum(0, h)
        for kind in range(4, 8):
            reduce_copy(kind, h).wait_recv()
            total = total + rrecv[kind, h, : size(h)].astype(F32)
        if h == 0:
            last = turn_back(total[MAIN:])
        else:
            total = jnp.concatenate([total, last], axis=0)
        total = unpack(total)
        high = total.astype(BF16)
        low = (total - high.astype(F32)).astype(BF16)
        back = dot_nn(weights_t, jnp.concatenate([high, low], axis=0)).astype(BF16)
        bsend[h] = back.reshape(n_slab, 16, BOX)
        for i in far_first:
            back_copy(h, i).start()
        own_copy(h).start()
        return last

    round_two(0)
    make_own(0)
    round_two(1)
    pair_copy(0).wait_recv()
    back_project(1, back_project(0))
    post_copy.wait()
    drain()
    for h in range(2):
        own_copy(h).wait()
        all_back(h).wait_send()
        all_back(h).wait_recv()


def on_device(n_slab, n_align, volume, images, orient, defocus, particle_counts):
    slots = images.shape[0]
    cols = 2 * BOX
    n_chunks = 8
    dma = pltpu.SemaphoreType.DMA
    hbm = pl.BlockSpec(memory_space=pltpu.HBM)
    planes, posterior = pl.pallas_call(
        functools.partial(kernel, n_slab, n_align),
        out_shape=(
            jax.ShapeDtypeStruct((2, n_slab, 16, BOX), BF16),
            jax.ShapeDtypeStruct((CAND, slots), F32),
        ),
        in_specs=[pl.BlockSpec(memory_space=pltpu.SMEM), hbm, hbm, hbm, hbm],
        out_specs=(hbm, hbm),
        scratch_shapes=[
            pltpu.VMEM((slots, ROWS, cols), BF16),
            pltpu.VMEM((ROWS, slots, cols + BOX), BF16),
            pltpu.VMEM((256, 256), BF16),
            pltpu.VMEM((16, ROWS, cols), BF16),
            pltpu.VMEM((CAND, slots), jnp.int32),
            pltpu.VMEM((slots,), BF16),
            pltpu.VMEM((slots, 128), F32),
            pltpu.VMEM((2, ROWS, 16, BOX), BF16),
            pltpu.VMEM((2, n_slab, 16, BOX), BF16),
            pltpu.VMEM((ROWS, 2, PIECE, 128), BF16),
            pltpu.VMEM((slots, 128), F32),
            pltpu.VMEM((slots, 128), F32),
            pltpu.VMEM((n_align, CAND, slots), F32),
            pltpu.VMEM((CHIPS, 2, PIECE, 128), F32),
            pltpu.VMEM((CHIPS, 2, PIECE, 128), BF16),
            pltpu.VMEM((CHIPS, 2, PIECE, 128), BF16),
            pltpu.VMEM((8, 2, PIECE, 128), BF16),
            pltpu.VMEM((8, 2, PIECE, 128), BF16),
            pltpu.VMEM((2, n_slab, 16, BOX), BF16),
            pltpu.VMEM((CAND, slots), F32),
            dma((n_chunks,)),
            dma((5,)),
            dma((2,)),
            dma((2,)),
            dma((8, 2)),
            dma((8, 2)),
            dma((CHIPS, 2)),
            dma((CHIPS, 2)),
            dma((1,)),
            dma((1,)),
            dma((CHIPS,)),
            dma((CHIPS,)),
            dma((8, 2)),
            dma((8, 2)),
            dma((2,)),
            dma((2,)),
        ],
        compiler_params=pltpu.CompilerParams(
            collective_id=0, has_side_effects=True, vmem_limit_bytes=60 * 1024 * 1024
        ),
    )(particle_counts, orient.T, defocus, volume, images)
    back_projection, posterior = pl.pallas_call(
        turn,
        out_shape=(
            jax.ShapeDtypeStruct((16, ROWS, cols), F32),
            jax.ShapeDtypeStruct((CAND, slots), F32),
        ),
        in_specs=[hbm, hbm],
        out_specs=(hbm, hbm),
        scratch_shapes=[
            pltpu.VMEM((2, n_slab, 16, BOX), BF16),
            pltpu.VMEM((16, ROWS, cols), F32),
            dma((5,)),
        ],
        compiler_params=pltpu.CompilerParams(vmem_limit_bytes=60 * 1024 * 1024),
    )(planes, posterior)
    return back_projection, posterior.T


def solution(mesh):
    return jax.shard_map(
        functools.partial(on_device, mesh.shape["slab"], mesh.shape["align"]),
        mesh=mesh,
        in_specs=(
            P("slab", "align", None),
            P("slab", "align", None),
            P("slab", None),
            P("slab"),
            P("slab"),
        ),
        out_specs=(P("slab", "align", None), P("slab", None)),
        check_vma=False,
    )
```
